256 devices in a mesh: tile: 128 (over y, z, x), slab: 2 (over core).
Axes of the slice: x: 4, y: 4, z: 8, core: 2. Of those that a mesh axis runs over, the one named last changes fastest.
Arguments:
- amplitudes: float32 [128, 256, 1600], P('tile', None, 'slab'), may hold values from -6 to 6
- integrals: float32 [8192, 40, 1600], P('tile', None, 'slab'), may hold values from -0.02734375 to 0.02734375
- tile_map: int32 [128], replicated, may hold values from 0 to 127, each once
- cd_ids: int32 [8192], P('tile'), may hold values from 0 to 127, as said below
- res_ids: int32 [8192], P('tile'), may hold values from 0 to 1
Outputs:
- residual: float32 [256, 40, 256], P('tile', None, 'slab')
The draws below stay inside these ranges and needn't reach their ends.
Inputs may be any that keep to these rules, and one draw needn't show every extreme that they name: `cd_ids`: the 64 entries of each aligned block of 64 name different amplitude tiles; one amplitude tile is named in every block.
All inputs are finite; a program needn't handle non-finite values.
Results may differ from the reference program's by a relative error of at most 0.0003.
Values sent between devices are 32-bit elements; how exact they have to be, the bound alone decides.
No kernel may reach another device: no remote copies, remote signals or barrier semaphores. Data moves between devices by JAX's collectives and lax.ppermute only.
A program may use at most 128 MiB of HBM per device.

```python
import jax
import jax.numpy as jnp
from jax import lax

VT = 40
VV = 1600
ROWS = 256
RD = 2
G = 128
HD = 64
NI = 8192


def draw_cd_ids(key, part):
    key = jax.random.fold_in(key, 11)
    first, second, third = jax.random.split(key, 3)
    popular = jax.random.randint(first, (G,), 0, 4)
    hottest = jax.random.randint(second, (), 0, G)
    noise = jax.random.randint(third, (G, G), 0, 1024)
    base = noise * (1 + popular)[None, :]
    base = jnp.where(jnp.arange(G)[None, :] == hottest, 8192, base)
    scores = base * G + jnp.arange(G, dtype=jnp.int32)[None, :]
    chosen = lax.top_k(scores, HD)[1]
    return chosen.reshape(-1).astype(jnp.int32)


def with_ends(drawn, stream_key, least, largest):
    extent = drawn.shape
    index_at = [jax.random.randint(jax.random.fold_in(stream_key, axis), (), 0, extent[axis]) for axis in range(len(extent))]
    drawn = drawn.at[tuple(index_at)].set(least)
    longest = extent.index(max(extent))
    index_at[longest] = (index_at[longest] + 1) % extent[longest]
    return drawn.at[tuple(index_at)].set(largest)


def block_levels(own_key, shape, cuts, low, high):
    def one(axis_at, blocks):
        draws = jax.random.uniform(jax.random.fold_in(jax.random.fold_in(own_key, 6), axis_at), (blocks,), jnp.float32, low / len(cuts), high / len(cuts))
        return jnp.repeat(jnp.exp(draws), shape[axis_at] // blocks).reshape((-1,) + (1,) * (len(shape) - axis_at - 1))

    loudness = one(*cuts[0])
    for cut in cuts[1:]:
        loudness = loudness * one(*cut)
    return loudness


def normal_values(key, shape, spread, most, pieces=(), kind=jnp.bfloat16):
    loudness = block_levels(key, shape, pieces, -0.22, 0.18) if pieces else 1.0
    values = jax.random.normal(key, shape, jnp.float32) * spread * loudness
    return jnp.minimum(jnp.maximum(values, -most), most).astype(kind)


def setup_inputs(seed: int = 0) -> dict:
    key_of = jax.random.split(jax.random.key(seed), 6)
    amplitudes = normal_values(key_of[0], (G, ROWS, VV), 1.0, 6.0, ((0, 128), (2, 2)), jnp.float32)
    integrals = normal_values(key_of[1], (NI, VT, VV), (VV * HD // RD) ** -0.5, 0.02734375, ((0, 128), (2, 2)), jnp.float32)
    tile_map = jax.random.permutation(key_of[2], G).astype(jnp.int32)
    cd_ids = draw_cd_ids(jax.random.fold_in(key_of[5], 71), 0)
    res_ids = with_ends(jax.random.randint(key_of[4], (NI,), 0, RD), jax.random.fold_in(key_of[4], 1), 0, RD - 1).astype(jnp.int32)
    return {"amplitudes": amplitudes, "integrals": integrals, "tile_map": tile_map, "cd_ids": cd_ids, "res_ids": res_ids}


def reference(amplitudes, integrals, tile_map, cd_ids, res_ids):
    inverse = jnp.zeros((G,), jnp.int32).at[tile_map].set(jnp.arange(G, dtype=jnp.int32))
    targets = jnp.arange(RD, dtype=jnp.int32)

    def one_owner(blocks):
        block_v, block_cd, block_res = blocks
        tiles = amplitudes[inverse[block_cd].astype(jnp.int32)]
        partial_value = jnp.einsum("hav,hrv->har", block_v, tiles, precision=lax.Precision.HIGHEST)
        select = (block_res[None, :] == targets[:, None]).astype(jnp.float32)
        return jnp.einsum("th,har->tar", select, partial_value, precision=lax.Precision.HIGHEST)

    summed = lax.map(one_owner, (integrals.reshape(G, HD, VT, VV), cd_ids.reshape(G, HD), res_ids.reshape(G, HD)))
    return summed.reshape(G * RD, VT, ROWS)
```

```python
import jax
import jax.numpy as jnp
from jax import lax
from jax.sharding import Mesh, PartitionSpec as P

RD = 2
PLANE = ("y", "x")
TILE = ("y", "z", "x")


def body(amplitudes, integrals, tile_map, cd_ids, res_ids):
    cell = lax.axis_size(PLANE)
    tiles, rows, depth = integrals.shape
    wide = amplitudes.shape[1]
    part = depth // cell
    peers = tile_map.shape[0]
    positions = jnp.arange(peers, dtype=jnp.int32)
    owner = jnp.sum(jnp.where(tile_map[None, :] == cd_ids[:, None], positions[None, :], 0), axis=1)
    meta = lax.all_gather(jnp.stack([owner, res_ids]), PLANE)
    owners, targets = meta[:, 0], meta[:, 1]
    own = amplitudes[0].reshape(wide, cell, part).transpose(1, 2, 0)
    own = lax.all_to_all(own, PLANE, split_axis=0, concat_axis=0, tiled=True)
    held = lax.all_gather(own, "z")
    held = held.reshape(lax.axis_size("z"), lax.axis_size("y"), lax.axis_size("x"), part, wide)
    held = held.transpose(1, 0, 2, 3, 4).reshape(peers, part, wide)
    sent = integrals.reshape(tiles, rows, cell, part).transpose(2, 1, 0, 3).reshape(cell, rows, tiles * part)
    got = lax.all_to_all(sent, PLANE, split_axis=0, concat_axis=0, tiled=True)
    def one(block):
        own_rows, own_targets, block_v = block
        picked = held[own_rows].reshape(tiles * part, wide)
        select = own_targets[None, :] == jnp.arange(RD, dtype=jnp.int32)[:, None]
        select = jnp.repeat(select, part, axis=1)
        masked = jnp.where(select[:, None, :], block_v[None], 0.0).reshape(RD * rows, tiles * part)
        return jnp.dot(masked, picked, precision=lax.Precision.HIGHEST)

    sums = lax.map(one, (owners, targets, got))
    cores = lax.axis_size("slab")
    sums = sums.reshape(cell, RD * rows, cores, wide // cores).transpose(0, 2, 1, 3)
    sums = sums.reshape(cell * cores, RD * rows, wide // cores)
    back = lax.all_to_all(sums, PLANE + ("slab",), split_axis=0, concat_axis=0, tiled=True)
    return jnp.sum(back, axis=0).reshape(RD, rows, wide // cores)


def solution(mesh):
    grid = Mesh(mesh.devices.reshape(4, 8, 4, 2), ("y", "z", "x", "slab"))
    placed = (P(TILE, None, "slab"), P(TILE, None, "slab"), P(), P(TILE), P(TILE))
    return jax.shard_map(
        body, mesh=grid, in_specs=placed, out_specs=P(TILE, None, "slab"), check_vma=False
    )
```

```python
import functools

import jax
import jax.numpy as jnp
from jax import lax
from jax.experimental import pallas as pl
from jax.experimental.pallas import tpu as pltpu
from jax.sharding import Mesh, PartitionSpec as P

RD = 2
PLANE = ("y", "x")
TILE = ("y", "z", "x")
LANES = 128
PITCH = 64
CHUNKS = ((0, 32), (32, 8))
VMEM = 56 * 1024 * 1024


def lane_ids():
    return lax.broadcasted_iota(jnp.int32, (8, LANES), 1)


def cut_kernel(part, v_ref, out_ref):
    tiles, _, depth = v_ref.shape
    cells = out_ref.shape[0]
    lane = lane_ids()
    full = depth // LANES

    def source(h, q):
        if q < full:
            return v_ref[h, :, q * LANES : (q + 1) * LANES]
        rest = v_ref[h, :, full * LANES : depth]
        return jnp.concatenate([rest, jnp.zeros((8, LANES - rest.shape[1]), rest.dtype)], axis=1)

    for c in range(cells):
        rolled = {}
        for j in range(tiles * part // LANES):
            made = None
            at = j * LANES
            while at < (j + 1) * LANES:
                h, v = divmod(at, part)
                q, o = divmod(c * part + v, LANES)
                run = min(part - v, LANES - o, (j + 1) * LANES - at)
                key = (h, q)
                if key not in rolled:
                    shift = (part * (h - c)) % LANES
                    rolled[key] = pltpu.roll(source(h, q), shift, 1) if shift else source(h, q)
                made = rolled[key] if made is None else jnp.where(lane >= at - j * LANES, rolled[key], made)
                at += run
            out_ref[c, :, j * LANES : (j + 1) * LANES] = made


def cut(integrals, cells, start, rows):
    tiles, _, depth = integrals.shape
    part = depth // cells
    return pl.pallas_call(
        functools.partial(cut_kernel, part),
        grid=(rows // 8,),
        in_specs=[pl.BlockSpec((tiles, 8, depth), lambda i: (0, i + start // 8, 0))],
        out_specs=pl.BlockSpec((cells, 8, tiles * part), lambda i: (0, i, 0)),
        out_shape=jax.ShapeDtypeStruct((cells, rows, tiles * part), jnp.float32),
        compiler_params=pltpu.CompilerParams(vmem_limit_bytes=VMEM),
        cost_estimate=pl.CostEstimate(flops=0, bytes_accessed=tiles * rows * depth * 8, transcendentals=0),
    )(integrals)


def split_kernel(part, t_ref, high_ref, low_ref):
    row = lax.broadcasted_iota(jnp.int32, (56, t_ref.shape[2]), 0)
    for s in range(t_ref.shape[0]):
        value = jnp.where(row < part, t_ref[s], 0.0)
        value = jnp.concatenate([value, jnp.zeros((PITCH - 56, value.shape[1]), value.dtype)], axis=0)
        high = value.astype(jnp.bfloat16)
        high_ref[s] = high
        low_ref[s] = (value - high.astype(jnp.float32)).astype(jnp.bfloat16)


def split(held, part):
    peers, rows, wide = held.shape
    block = 16
    shape = jax.ShapeDtypeStruct((peers, PITCH, wide), jnp.bfloat16)
    return pl.pallas_call(
        functools.partial(split_kernel, part),
        grid=(peers // block,),
        in_specs=[pl.BlockSpec((block, rows, wide), lambda i: (i, 0, 0))],
        out_specs=[pl.BlockSpec((block, PITCH, wide), lambda i: (i, 0, 0))] * 2,
        out_shape=(shape, shape),
        compiler_params=pltpu.CompilerParams(vmem_limit_bytes=VMEM),
        cost_estimate=pl.CostEstimate(flops=0, bytes_accessed=peers * wide * 480, transcendentals=0),
    )(held)


def ladder_kernel(part, own_ref, v_ref, mask_ref, high_ref, low_ref, out_ref):
    d = pl.program_id(0)
    rows = v_ref.shape[1]
    lane = lax.broadcasted_iota(jnp.int32, (rows, LANES), 1)
    total = jnp.zeros((2 * rows, high_ref.shape[2]), jnp.float32)

    def piece(h):
        q, o = divmod(part * h, LANES)
        base = PITCH * (h % 2)
        shift = (base - o) % LANES
        first = v_ref[0, :, q * LANES : (q + 1) * LANES]
        first = pltpu.roll(first, shift, 1) if shift else first
        if o + part <= LANES:
            return first
        second = v_ref[0, :, (q + 1) * LANES : (q + 2) * LANES]
        second = pltpu.roll(second, shift, 1) if shift else second
        return jnp.where(lane < base + LANES - o, first, second)

    for j in range(mask_ref.shape[1]):
        halves = []
        for k in range(2):
            h = 4 * j + 2 * k
            halves.append(jnp.where(lane < PITCH, piece(h), piece(h + 1)))
        value = jnp.concatenate(halves, axis=1)
        zeroth = value * mask_ref[0, j : j + 1, :]
        value = jnp.concatenate([zeroth, value - zeroth], axis=0)
        high = value.astype(jnp.bfloat16)
        low = (value - high.astype(jnp.float32)).astype(jnp.bfloat16)
        at = [own_ref[d, 4 * j + i] for i in range(4)]
        t_high = jnp.concatenate([high_ref[s] for s in at], axis=0)
        t_low = jnp.concatenate([low_ref[s] for s in at], axis=0)
        total += jnp.dot(high, t_high, preferred_element_type=jnp.float32)
        total += jnp.dot(low, t_high, preferred_element_type=jnp.float32)
        total += jnp.dot(high, t_low, preferred_element_type=jnp.float32)
    out_ref[0] = total[:, :LANES]
    out_ref[1] = total[:, LANES:]


def ladder(owners, got, masks, high, low, part):
    cell, rows, width = got.shape
    peers, _, wide = high.shape
    cores = wide // LANES
    groups = masks.shape[1]
    whole = pl.BlockSpec((peers, PITCH, wide), lambda d, own: (0, 0, 0), pipeline_mode=pl.Buffered(1))
    return pl.pallas_call(
        functools.partial(ladder_kernel, part),
        grid_spec=pltpu.PrefetchScalarGridSpec(
            num_scalar_prefetch=1,
            grid=(cell,),
            in_specs=[
                pl.BlockSpec((1, rows, width), lambda d, own: (d, 0, 0)),
                pl.BlockSpec((1, groups, 4 * PITCH), lambda d, own: (d, 0, 0)),
                whole,
                whole,
            ],
            out_specs=pl.BlockSpec((cores, RD * rows, LANES), lambda d, own: (d, 0, 0)),
        ),
        out_shape=jax.ShapeDtypeStruct((cell * cores, RD * rows, LANES), jnp.float32),
        compiler_params=pltpu.CompilerParams(vmem_limit_bytes=VMEM),
        cost_estimate=pl.CostEstimate(
            flops=6 * 2 * rows * cell * groups * 4 * PITCH * wide, bytes_accessed=4 * got.size + 4 * high.size, transcendentals=0
        ),
    )(owners, got, masks, high, low)


def exchange(value, axes):
    return lax.all_to_all(value, axes, split_axis=0, concat_axis=0, tiled=True)


def body(amplitudes, integrals, tile_map, cd_ids, res_ids):
    cell = lax.axis_size(PLANE)
    tiles, rows, depth = integrals.shape
    wide = amplitudes.shape[1]
    part = depth // cell
    peers = tile_map.shape[0]
    across, along = lax.axis_size("x"), lax.axis_size("z")
    positions = jnp.arange(peers, dtype=jnp.int32)
    at_x, at_z, at_y = positions % across, positions // across % along, positions // (across * along)
    slots = (at_z * lax.axis_size("y") + at_y) * across + at_x
    owner = jnp.sum(jnp.where(tile_map[None, :] == cd_ids[:, None], slots[None, :], 0), axis=1)
    ids = jnp.concatenate([owner, res_ids]).astype(jnp.float32)
    tail = jnp.zeros((56 - part, wide), jnp.float32).at[0, : 2 * tiles].set(ids)
    own = amplitudes[0].T.reshape(cell, part, wide)
    own = jnp.concatenate([own, jnp.broadcast_to(tail[None], (cell,) + tail.shape)], axis=1)
    own = exchange(own, PLANE)
    meta = own[:, part, : 2 * tiles].astype(jnp.int32)
    owners, targets = meta[:, :tiles], meta[:, tiles:]
    masks = jnp.repeat((targets == 0).astype(jnp.float32), PITCH, axis=1).reshape(cell, tiles // 4, 4 * PITCH)
    held = lax.all_gather(own, "z").reshape(peers, 56, wide)
    high, low = split(held, part)
    parts = []
    for start, count in CHUNKS:
        got = exchange(cut(integrals, cell, start, count), PLANE)
        sums = ladder(owners, got, masks, high, low, part)
        back = exchange(sums, PLANE + ("slab",))
        parts.append(jnp.sum(back, axis=0).reshape(RD, count, LANES))
    return jnp.concatenate(parts, axis=1)


def solution(mesh):
    grid = Mesh(mesh.devices.reshape(4, 8, 4, 2), ("y", "z", "x", "slab"))
    placed = (P(TILE, None, "slab"), P(TILE, None, "slab"), P(), P(TILE), P(TILE))
    return jax.shard_map(
        body, mesh=grid, in_specs=placed, out_specs=P(TILE, None, "slab"), check_vma=False
    )
```

```python
import functools

import jax
import jax.numpy as jnp
from jax import lax
from jax.experimental import pallas as pl
from jax.experimental.pallas import tpu as pltpu
from jax.sharding import Mesh, PartitionSpec as P

RD = 2
PLANE = ("y", "x")
TILE = ("y", "z", "x")
LANES = 128
PITCH = 64
PADDED = 56
VMEM = 20 * 1024 * 1024


def pack_kernel(part, tiles, shape, map_ref, cd_ref, res_ref, t_ref, out_ref, order_ref):
    size_y, size_z, size_x = shape
    square = (LANES, LANES)
    lane = lax.broadcasted_iota(jnp.int32, square, 1)
    row = lax.broadcasted_iota(jnp.int32, square, 0)

    def down(values):
        return jnp.transpose(jnp.broadcast_to(values, square))

    def wide(ref):
        values = ref[...].astype(jnp.float32)
        return jnp.concatenate([values, jnp.zeros((1, LANES - values.shape[1]), jnp.float32)], axis=1)

    cd, target = wide(cd_ref), wide(res_ref)
    at_x, at_z, at_y = row % size_x, row // size_x % size_z, row // (size_x * size_z)
    slot = ((at_z * size_y + at_y) * size_x + at_x).astype(jnp.float32)
    match = down(map_ref[...].astype(jnp.float32)) == cd
    owner = jnp.sum(jnp.where(match, slot, 0.0), axis=0, keepdims=True)
    key = target * tiles + lane[:1].astype(jnp.float32)
    rank = jnp.sum(jnp.where((down(key) < key) & (row < tiles), 1.0, 0.0), axis=0, keepdims=True)
    here = (down(rank) == lane.astype(jnp.float32)) & (row < tiles)
    order = jnp.sum(jnp.where(here, row.astype(jnp.float32), 0.0), axis=0, keepdims=True)
    owner = jnp.sum(jnp.where(here, down(owner), 0.0), axis=0, keepdims=True)
    zeros = jnp.sum(jnp.where((lane[:1] < tiles) & (target == 0.0), 1.0, 0.0), axis=1, keepdims=True)
    order_ref[...] = order.astype(jnp.int32)
    ids = jnp.where(lane[:1] == tiles, zeros, owner)
    tail = jnp.zeros((PADDED - part, t_ref.shape[1]), jnp.float32)
    for c in range(out_ref.shape[0]):
        out_ref[c, :part, :] = t_ref[c * part : (c + 1) * part, :]
        out_ref[c, part:, :] = tail
        out_ref[c, part : part + 1, :LANES] = ids


def pack(tile_map, cd_ids, res_ids, turned, cell, shape):
    depth, wide = turned.shape
    part = depth // cell
    tiles = cd_ids.shape[0]
    return pl.pallas_call(
        functools.partial(pack_kernel, part, tiles, shape),
        out_shape=(
            jax.ShapeDtypeStruct((cell, PADDED, wide), jnp.float32),
            jax.ShapeDtypeStruct((1, LANES), jnp.int32),
        ),
        compiler_params=pltpu.CompilerParams(vmem_limit_bytes=VMEM),
        cost_estimate=pl.CostEstimate(flops=0, bytes_accessed=depth * wide * 8, transcendentals=0),
    )(tile_map[None], cd_ids[None], res_ids[None], turned)


def cut_kernel(part, order_ref, v_ref, out_ref):
    tiles, _, depth = v_ref.shape
    cells = out_ref.shape[0]
    lane = lax.broadcasted_iota(jnp.int32, (8, LANES), 1)
    full = depth // LANES
    order = [order_ref[0, h] for h in range(tiles)]

    def source(h, q):
        if q < full:
            return v_ref[order[h], :, q * LANES : (q + 1) * LANES]
        rest = v_ref[order[h], :, full * LANES : depth]
        return jnp.concatenate([rest, jnp.zeros((8, LANES - rest.shape[1]), rest.dtype)], axis=1)

    for c in range(cells):
        rolled = {}
        for j in range(tiles * part // LANES):
            made = None
            at = j * LANES
            while at < (j + 1) * LANES:
                h, v = divmod(at, part)
                q, o = divmod(c * part + v, LANES)
                run = min(part - v, LANES - o, (j + 1) * LANES - at)
                key = (h, q)
                if key not in rolled:
                    shift = (part * (h - c)) % LANES
                    rolled[key] = pltpu.roll(source(h, q), shift, 1) if shift else source(h, q)
                made = rolled[key] if made is None else jnp.where(lane >= at - j * LANES, rolled[key], made)
                at += run
            out_ref[c, :, j * LANES : (j + 1) * LANES] = made


def cut(order, integrals, cells):
    tiles, rows, depth = integrals.shape
    part = depth // cells
    return pl.pallas_call(
        functools.partial(cut_kernel, part),
        grid_spec=pltpu.PrefetchScalarGridSpec(
            num_scalar_prefetch=1,
            grid=(rows // 8,),
            in_specs=[pl.BlockSpec((tiles, 8, depth), lambda i, order: (0, i, 0))],
            out_specs=pl.BlockSpec((cells, 8, tiles * part), lambda i, order: (0, i, 0)),
        ),
        out_shape=jax.ShapeDtypeStruct((cells, rows, tiles * part), jnp.float32),
        compiler_params=pltpu.CompilerParams(vmem_limit_bytes=VMEM),
        cost_estimate=pl.CostEstimate(flops=0, bytes_accessed=tiles * rows * depth * 8, transcendentals=0),
    )(order, integrals)


def split_kernel(part, t_ref, high_ref, low_ref):
    row = lax.broadcasted_iota(jnp.int32, (PADDED, t_ref.shape[2]), 0)
    for s in range(t_ref.shape[0]):
        value = jnp.where(row < part, t_ref[s], 0.0)
        value = jnp.concatenate([value, jnp.zeros((PITCH - PADDED, value.shape[1]), value.dtype)], axis=0)
        high = value.astype(jnp.bfloat16)
        high_ref[s] = high
        low_ref[s] = (value - high.astype(jnp.float32)).astype(jnp.bfloat16)


def split(held, part):
    peers, rows, wide = held.shape
    block = 16
    shape = jax.ShapeDtypeStruct((peers, PITCH, wide), jnp.bfloat16)
    return pl.pallas_call(
        functools.partial(split_kernel, part),
        grid=(peers // block,),
        in_specs=[pl.BlockSpec((block, rows, wide), lambda i: (i, 0, 0))],
        out_specs=[pl.BlockSpec((block, PITCH, wide), lambda i: (i, 0, 0))] * 2,
        out_shape=(shape, shape),
        compiler_params=pltpu.CompilerParams(vmem_limit_bytes=VMEM),
        cost_estimate=pl.CostEstimate(flops=0, bytes_accessed=peers * wide * 480, transcendentals=0),
    )(held)


def ladder_kernel(part, meta_ref, v_ref, high_ref, low_ref, out_ref, kept_ref, major_ref, minor_ref):
    d = pl.program_id(0)
    rows = v_ref.shape[1]
    tiles = v_ref.shape[2] // part
    groups = tiles // 4
    lane = lax.broadcasted_iota(jnp.int32, (rows, LANES), 1)
    spread = lax.broadcasted_iota(jnp.int32, (rows, 4 * PITCH), 1)
    zeros = meta_ref[d, tiles]
    mixed = jnp.minimum(zeros // 4, groups - 1)
    edge = (zeros - 4 * mixed) * PITCH

    def piece(h):
        q, o = divmod(part * h, LANES)
        base = PITCH * (h % 2)
        shift = (base - o) % LANES
        first = v_ref[0, :, q * LANES : (q + 1) * LANES]
        first = pltpu.roll(first, shift, 1) if shift else first
        if o + part <= LANES:
            return first
        second = v_ref[0, :, (q + 1) * LANES : (q + 2) * LANES]
        second = pltpu.roll(second, shift, 1) if shift else second
        return jnp.where(lane < base + LANES - o, first, second)

    def add(value, j, target):
        rest = value - value.astype(jnp.bfloat16).astype(jnp.float32)
        both = jnp.concatenate([value, rest], axis=0).astype(jnp.bfloat16)
        at = [meta_ref[d, 4 * j + i] for i in range(4)]
        t_high = jnp.concatenate([high_ref[s] for s in at], axis=0)
        t_low = jnp.concatenate([low_ref[s] for s in at], axis=0)
        major_ref[target] += jnp.dot(both, t_high, preferred_element_type=jnp.float32)
        minor_ref[target] += jnp.dot(both[:rows], t_low, preferred_element_type=jnp.float32)

    major_ref[...] = jnp.zeros(major_ref.shape, jnp.float32)
    minor_ref[...] = jnp.zeros(minor_ref.shape, jnp.float32)
    for j in range(groups):
        halves = []
        for k in range(2):
            h = 4 * j + 2 * k
            halves.append(jnp.where(lane < PITCH, piece(h), piece(h + 1)))
        value = jnp.concatenate(halves, axis=1)
        kept_ref[j] = value
        start = jnp.where(mixed == j, edge, 0)
        add(jnp.where(spread >= start, value, 0.0), j, jnp.where(mixed <= j, 1, 0))
    add(jnp.where(spread < edge, kept_ref[mixed], 0.0), mixed, 0)
    for t in range(RD):
        total = major_ref[t, :rows] + major_ref[t, rows:] + minor_ref[t]
        for k in range(out_ref.shape[0]):
            out_ref[k, 0, t * rows : (t + 1) * rows, :] = total[:, k * LANES : (k + 1) * LANES]


def ladder(meta, got, high, low, part):
    cell, rows, width = got.shape
    peers, _, wide = high.shape
    cores = wide // LANES
    groups = width // part // 4
    whole = pl.BlockSpec((peers, PITCH, wide), lambda d, meta: (0, 0, 0), pipeline_mode=pl.Buffered(1))
    return pl.pallas_call(
        functools.partial(ladder_kernel, part),
        grid_spec=pltpu.PrefetchScalarGridSpec(
            num_scalar_prefetch=1,
            grid=(cell,),
            in_specs=[pl.BlockSpec((1, rows, width), lambda d, meta: (d, 0, 0)), whole, whole],
            out_specs=pl.BlockSpec((cores, 1, RD * rows, LANES), lambda d, meta: (0, d, 0, 0)),
            scratch_shapes=[
                pltpu.VMEM((groups, rows, 4 * PITCH), jnp.float32),
                pltpu.VMEM((RD, 2 * rows, wide), jnp.float32),
                pltpu.VMEM((RD, rows, wide), jnp.float32),
            ],
        ),
        out_shape=jax.ShapeDtypeStruct((cores, cell, RD * rows, LANES), jnp.float32),
        compiler_params=pltpu.CompilerParams(vmem_limit_bytes=VMEM),
        cost_estimate=pl.CostEstimate(
            flops=6 * rows * cell * groups * 4 * PITCH * wide, bytes_accessed=4 * got.size + 4 * high.size, transcendentals=0
        ),
    )(meta, got, high, low)


def exchange(value, axes):
    return lax.all_to_all(value, axes, split_axis=0, concat_axis=0, tiled=True)


def body(amplitudes, integrals, tile_map, cd_ids, res_ids):
    cell = lax.axis_size(PLANE)
    tiles, rows, depth = integrals.shape
    wide = amplitudes.shape[1]
    part = depth // cell
    peers = tile_map.shape[0]
    shape = tuple(lax.axis_size(a) for a in TILE)
    own, order = pack(tile_map, cd_ids, res_ids, amplitudes[0].T, cell, shape)
    own = exchange(own, PLANE)
    shared = lax.all_gather(own, "z")
    meta = own[:, part, :LANES].astype(jnp.int32)
    sent, meta = lax.optimization_barrier((cut(order, integrals, cell), meta))
    got = exchange(sent, PLANE)
    got, shared, meta = lax.optimization_barrier((got, shared, meta))
    high, low = split(shared.reshape(peers, PADDED, wide), part)
    sums = ladder(meta, got, high, low, part)
    core = lax.axis_index("slab")
    mine = lax.dynamic_index_in_dim(sums, core, 0, keepdims=False)
    other = lax.dynamic_index_in_dim(sums, 1 - core, 0, keepdims=False)
    mine += lax.ppermute(other, "slab", [(0, 1), (1, 0)])
    back = exchange(mine, PLANE)
    return jnp.sum(back, axis=0).reshape(RD, rows, LANES)


def solution(mesh):
    grid = Mesh(mesh.devices.reshape(4, 8, 4, 2), TILE + ("slab",))
    placed = (P(TILE, None, "slab"), P(TILE, None, "slab"), P(), P(TILE), P(TILE))
    return jax.shard_map(
        body, mesh=grid, in_specs=placed, out_specs=P(TILE, None, "slab"), check_vma=False
    )
```

```python
import functools

import jax
import jax.numpy as jnp
from jax import lax
from jax.experimental import pallas as pl
from jax.experimental.pallas import tpu as pltpu
from jax.sharding import Mesh, PartitionSpec as P

RD = 2
PLANE = ("y", "x")
TILE = ("y", "z", "x")
LANES = 128
PITCH = 64
PADDED = 56
VMEM = 56 * 1024 * 1024
FIRST = 56


def pack_kernel(part, tiles, shape, map_ref, cd_ref, res_ref, t_ref, out_ref):
    size_y, size_z, size_x = shape
    square = (LANES, LANES)
    row = lax.broadcasted_iota(jnp.int32, square, 0)
    at_x, at_z, at_y = row % size_x, row // size_x % size_z, row // (size_x * size_z)
    slot = ((at_z * size_y + at_y) * size_x + at_x).astype(jnp.float32)
    ids = jnp.transpose(jnp.broadcast_to(map_ref[...].astype(jnp.float32), square))
    match = ids[:, :tiles] == cd_ref[...].astype(jnp.float32)
    owner = jnp.sum(jnp.where(match, slot[:, :tiles], 0.0), axis=0, keepdims=True)
    ids = jnp.concatenate([owner, res_ref[...].astype(jnp.float32)], axis=1)
    tail = jnp.zeros((PADDED - part, t_ref.shape[1]), jnp.float32)
    for c in range(out_ref.shape[0]):
        out_ref[c, :part, :] = t_ref[c * part : (c + 1) * part, :]
        out_ref[c, part:, :] = tail
        out_ref[c, part : part + 1, : 2 * tiles] = ids


def pack(tile_map, cd_ids, res_ids, turned, cell, shape):
    depth, wide = turned.shape
    part = depth // cell
    tiles = cd_ids.shape[0]
    return pl.pallas_call(
        functools.partial(pack_kernel, part, tiles, shape),
        out_shape=jax.ShapeDtypeStruct((cell, PADDED, wide), jnp.float32),
        compiler_params=pltpu.CompilerParams(vmem_limit_bytes=VMEM),
        cost_estimate=pl.CostEstimate(flops=0, bytes_accessed=depth * wide * 8, transcendentals=0),
    )(tile_map[None], cd_ids[None], res_ids[None], turned)


def cut_kernel(part, spans, v_ref, *out_refs):
    depth = v_ref.shape[2]
    lane = lax.broadcasted_iota(jnp.int32, (8, LANES), 1)
    full = depth // LANES

    def source(h, q):
        if q < full:
            return v_ref[h, :, q * LANES : (q + 1) * LANES]
        rest = v_ref[h, :, full * LANES : depth]
        return jnp.concatenate([rest, jnp.zeros((8, LANES - rest.shape[1]), rest.dtype)], axis=1)

    for (begin, count), out_ref in zip(spans, out_refs, strict=True):
        for c in range(out_ref.shape[0]):
            rolled = {}
            for j in range(out_ref.shape[2] // LANES):
                made = None
                at = j * LANES
                while at < min((j + 1) * LANES, count * part):
                    h, v = divmod(at, part)
                    q, o = divmod(c * part + v, LANES)
                    run = min(part - v, LANES - o, (j + 1) * LANES - at)
                    key = (h, q)
                    if key not in rolled:
                        shift = (part * (h - c)) % LANES
                        value = source(begin + h, q)
                        rolled[key] = pltpu.roll(value, shift, 1) if shift else value
                    made = rolled[key] if made is None else jnp.where(lane >= at - j * LANES, rolled[key], made)
                    at += run
                out_ref[c, :, j * LANES : (j + 1) * LANES] = made


def cut(integrals, cells, spans):
    tiles, rows, depth = integrals.shape
    part = depth // cells
    widths = [pl.cdiv(count * part, LANES) * LANES for _, count in spans]
    return pl.pallas_call(
        functools.partial(cut_kernel, part, spans),
        grid=(rows // 8,),
        in_specs=[pl.BlockSpec((tiles, 8, depth), lambda i: (0, i, 0))],
        out_specs=[pl.BlockSpec((cells, 8, width), lambda i: (0, i, 0)) for width in widths],
        out_shape=[jax.ShapeDtypeStruct((cells, rows, width), jnp.float32) for width in widths],
        compiler_params=pltpu.CompilerParams(vmem_limit_bytes=VMEM),
        cost_estimate=pl.CostEstimate(flops=0, bytes_accessed=tiles * rows * depth * 8, transcendentals=0),
    )(integrals)


def split_kernel(part, t_ref, high_ref, low_ref):
    row = lax.broadcasted_iota(jnp.int32, (PADDED, t_ref.shape[2]), 0)
    for s in range(t_ref.shape[0]):
        value = jnp.where(row < part, t_ref[s], 0.0)
        value = jnp.concatenate([value, jnp.zeros((PITCH - PADDED, value.shape[1]), value.dtype)], axis=0)
        high = value.astype(jnp.bfloat16)
        high_ref[s] = high
        low_ref[s] = (value - high.astype(jnp.float32)).astype(jnp.bfloat16)


def split(held, part):
    peers, rows, wide = held.shape
    block = 16
    shape = jax.ShapeDtypeStruct((peers, PITCH, wide), jnp.bfloat16)
    return pl.pallas_call(
        functools.partial(split_kernel, part),
        grid=(peers // block,),
        in_specs=[pl.BlockSpec((block, rows, wide), lambda i: (i, 0, 0))],
        out_specs=[pl.BlockSpec((block, PITCH, wide), lambda i: (i, 0, 0))] * 2,
        out_shape=(shape, shape),
        compiler_params=pltpu.CompilerParams(vmem_limit_bytes=VMEM),
        cost_estimate=pl.CostEstimate(flops=0, bytes_accessed=peers * wide * 480, transcendentals=0),
    )(held)


def ladder_kernel(part, span, step, meta_ref, v_ref, high_ref, low_ref, *refs):
    d = pl.program_id(0)
    before_ref, out_ref = refs if len(refs) == 2 else (None, refs[0])
    rows = v_ref.shape[1]
    wide = high_ref.shape[2]
    begin, count = span
    tiles = meta_ref.shape[1] // 2
    lane = lax.broadcasted_iota(jnp.int32, (rows, LANES), 1)
    lane_row = lax.broadcasted_iota(jnp.int32, (1, LANES), 1)

    def piece(h):
        q, o = divmod(part * h, LANES)
        base = PITCH * (h % 2)
        shift = (base - o) % LANES
        first = v_ref[0, :, q * LANES : (q + 1) * LANES]
        first = pltpu.roll(first, shift, 1) if shift else first
        if o + part <= LANES:
            return first
        second = v_ref[0, :, (q + 1) * LANES : (q + 2) * LANES]
        second = pltpu.roll(second, shift, 1) if shift else second
        return jnp.where(lane < base + LANES - o, first, second)

    def is_zeroth(h):
        return (1 - meta_ref[d, tiles + begin + h]).astype(jnp.float32)

    total = jnp.zeros((4 * rows, wide), jnp.float32)
    minor = jnp.zeros((2 * rows, wide), jnp.float32)
    for g in range(0, count, step):
        both = []
        for h in range(g, g + step, 2):
            value = jnp.where(lane < PITCH, piece(h), piece(h + 1))
            zeroth = value * jnp.where(lane_row < PITCH, is_zeroth(h), is_zeroth(h + 1))
            value = jnp.concatenate([zeroth, value - zeroth], axis=0)
            rest = value - value.astype(jnp.bfloat16).astype(jnp.float32)
            both.append(jnp.concatenate([value, rest], axis=0).astype(jnp.bfloat16))
        both = jnp.concatenate(both, axis=1)
        at = [meta_ref[d, begin + h] for h in range(g, g + step)]
        t_high = jnp.concatenate([high_ref[s] for s in at], axis=0)
        t_low = jnp.concatenate([low_ref[s] for s in at], axis=0)
        total += jnp.dot(both, t_high, preferred_element_type=jnp.float32)
        minor += jnp.dot(both[: 2 * rows], t_low, preferred_element_type=jnp.float32)
    total = total[: 2 * rows] + total[2 * rows :] + minor
    for k in range(out_ref.shape[0]):
        value = total[:, k * LANES : (k + 1) * LANES]
        out_ref[k, 0] = value if before_ref is None else before_ref[k, 0] + value


def ladder(meta, got, high, low, part, span, step, before=None):
    cell, rows, width = got.shape
    peers, _, wide = high.shape
    cores = wide // LANES
    whole = pl.BlockSpec((peers, PITCH, wide), lambda d, meta: (0, 0, 0), pipeline_mode=pl.Buffered(1))
    sums = pl.BlockSpec((cores, 1, RD * rows, LANES), lambda d, meta: (0, d, 0, 0))
    return pl.pallas_call(
        functools.partial(ladder_kernel, part, span, step),
        grid_spec=pltpu.PrefetchScalarGridSpec(
            num_scalar_prefetch=1,
            grid=(cell,),
            in_specs=[pl.BlockSpec((1, rows, width), lambda d, meta: (d, 0, 0)), whole, whole]
            + ([] if before is None else [sums]),
            out_specs=sums,
        ),
        out_shape=jax.ShapeDtypeStruct((cores, cell, RD * rows, LANES), jnp.float32),
        compiler_params=pltpu.CompilerParams(vmem_limit_bytes=VMEM),
        cost_estimate=pl.CostEstimate(
            flops=12 * RD * rows * cell * span[1] * PITCH * wide, bytes_accessed=4 * got.size + 4 * high.size, transcendentals=0
        ),
    )(meta, got, high, low, *(() if before is None else (before,)))


def exchange(value, axes):
    return lax.all_to_all(value, axes, split_axis=0, concat_axis=0, tiled=True)


def body(amplitudes, integrals, tile_map, cd_ids, res_ids):
    cell = lax.axis_size(PLANE)
    tiles, rows, depth = integrals.shape
    wide = amplitudes.shape[1]
    part = depth // cell
    peers = tile_map.shape[0]
    shape = tuple(lax.axis_size(a) for a in TILE)
    spans = ((0, FIRST), (FIRST, tiles - FIRST))
    own = exchange(pack(tile_map, cd_ids, res_ids, amplitudes[0].T, cell, shape), PLANE)
    sent, late = cut(integrals, cell, spans)
    meta = own[:, part, : 2 * tiles].astype(jnp.int32)
    own, sent, late = lax.optimization_barrier((own, sent, late))
    shared = lax.all_gather(own, "z")
    sent, meta, core = lax.optimization_barrier((sent, meta, lax.axis_index("slab")))
    got = exchange(sent, PLANE)
    got, late, shared, meta, core = lax.optimization_barrier((got, late, shared, meta, core))
    later = exchange(late, PLANE)
    high, low = split(shared.reshape(peers, PADDED, wide), part)
    sums = ladder(meta, got, high, low, part, spans[0], 8)
    sums = ladder(meta, later, high, low, part, spans[1], 8, sums)
    mine = lax.dynamic_index_in_dim(sums, core, 0, keepdims=False)
    other = lax.dynamic_index_in_dim(sums, 1 - core, 0, keepdims=False)
    mine += lax.ppermute(other, "slab", [(0, 1), (1, 0)])
    back = exchange(mine, PLANE)
    return jnp.sum(back, axis=0).reshape(RD, rows, LANES)


def solution(mesh):
    grid = Mesh(mesh.devices.reshape(4, 8, 4, 2), TILE + ("slab",))
    placed = (P(TILE, None, "slab"), P(TILE, None, "slab"), P(), P(TILE), P(TILE))
    return jax.shard_map(
        body, mesh=grid, in_specs=placed, out_specs=P(TILE, None, "slab"), check_vma=False
    )
```

```python
import functools

import jax
import jax.numpy as jnp
from jax import lax
from jax.experimental import pallas as pl
from jax.experimental.pallas import tpu as pltpu
from jax.sharding import Mesh, PartitionSpec as P

RD = 2
PLANE = ("y", "x")
TILE = ("y", "z", "x")
LANES = 128
PITCH = 64
PADDED = 56
VMEM = 56 * 1024 * 1024
FIRST = 56


def pack_kernel(part, tiles, shape, map_ref, cd_ref, res_ref, t_ref, out_ref):
    size_y, size_z, size_x = shape
    square = (LANES, LANES)
    row = lax.broadcasted_iota(jnp.int32, square, 0)
    at_x, at_z, at_y = row % size_x, row // size_x % size_z, row // (size_x * size_z)
    slot = ((at_z * size_y + at_y) * size_x + at_x).astype(jnp.float32)
    ids = jnp.transpose(jnp.broadcast_to(map_ref[...].astype(jnp.float32), square))
    match = ids[:, :tiles] == cd_ref[...].astype(jnp.float32)
    owner = jnp.sum(jnp.where(match, slot[:, :tiles], 0.0), axis=0, keepdims=True)
    ids = jnp.concatenate([owner, res_ref[...].astype(jnp.float32)], axis=1)
    tail = jnp.zeros((PADDED - part, t_ref.shape[1]), jnp.float32)
    for c in range(out_ref.shape[0]):
        out_ref[c, :part, :] = t_ref[c * part : (c + 1) * part, :]
        out_ref[c, part:, :] = tail
        out_ref[c, part : part + 1, : 2 * tiles] = ids


def pack(tile_map, cd_ids, res_ids, turned, cell, shape):
    depth, wide = turned.shape
    part = depth // cell
    tiles = cd_ids.shape[0]
    return pl.pallas_call(
        functools.partial(pack_kernel, part, tiles, shape),
        out_shape=jax.ShapeDtypeStruct((cell, PADDED, wide), jnp.float32),
        compiler_params=pltpu.CompilerParams(vmem_limit_bytes=VMEM),
        cost_estimate=pl.CostEstimate(flops=0, bytes_accessed=depth * wide * 8, transcendentals=0),
    )(tile_map[None], cd_ids[None], res_ids[None], turned)


def cut_kernel(part, spans, v_ref, *out_refs):
    depth = v_ref.shape[2]
    lane = lax.broadcasted_iota(jnp.int32, (8, LANES), 1)
    full = depth // LANES

    def source(h, q):
        if q < full:
            return v_ref[h, :, q * LANES : (q + 1) * LANES]
        rest = v_ref[h, :, full * LANES : depth]
        return jnp.concatenate([rest, jnp.zeros((8, LANES - rest.shape[1]), rest.dtype)], axis=1)

    for (begin, count), out_ref in zip(spans, out_refs, strict=True):
        for c in range(out_ref.shape[0]):
            rolled = {}
            for j in range(out_ref.shape[2] // LANES):
                made = None
                at = j * LANES
                while at < min((j + 1) * LANES, count * part):
                    h, v = divmod(at, part)
                    q, o = divmod(c * part + v, LANES)
                    run = min(part - v, LANES - o, (j + 1) * LANES - at)
                    key = (h, q)
                    if key not in rolled:
                        shift = (part * (h - c)) % LANES
                        value = source(begin + h, q)
                        rolled[key] = pltpu.roll(value, shift, 1) if shift else value
                    made = rolled[key] if made is None else jnp.where(lane >= at - j * LANES, rolled[key], made)
                    at += run
                out_ref[c, :, j * LANES : (j + 1) * LANES] = made


def cut(integrals, cells, spans):
    tiles, rows, depth = integrals.shape
    part = depth // cells
    widths = [pl.cdiv(count * part, LANES) * LANES for _, count in spans]
    return pl.pallas_call(
        functools.partial(cut_kernel, part, spans),
        grid=(rows // 8,),
        in_specs=[pl.BlockSpec((tiles, 8, depth), lambda i: (0, i, 0))],
        out_specs=[pl.BlockSpec((cells, 8, width), lambda i: (0, i, 0)) for width in widths],
        out_shape=[jax.ShapeDtypeStruct((cells, rows, width), jnp.float32) for width in widths],
        compiler_params=pltpu.CompilerParams(vmem_limit_bytes=VMEM),
        cost_estimate=pl.CostEstimate(flops=0, bytes_accessed=tiles * rows * depth * 8, transcendentals=0),
    )(integrals)


def contract(part, span, step, tiles, own, load, rows, high_ref, low_ref):
    wide = high_ref.shape[2]
    begin, count = span
    lane = lax.broadcasted_iota(jnp.int32, (rows, LANES), 1)
    lane_row = lax.broadcasted_iota(jnp.int32, (1, LANES), 1)

    def piece(h):
        q, o = divmod(part * h, LANES)
        base = PITCH * (h % 2)
        shift = (base - o) % LANES
        first = load(q)
        first = pltpu.roll(first, shift, 1) if shift else first
        if o + part <= LANES:
            return first
        second = load(q + 1)
        second = pltpu.roll(second, shift, 1) if shift else second
        return jnp.where(lane < base + LANES - o, first, second)

    def is_zeroth(h):
        return (1 - own(tiles + begin + h)).astype(jnp.float32)

    total = jnp.zeros((4 * rows, wide), jnp.float32)
    minor = jnp.zeros((2 * rows, wide), jnp.float32)
    for g in range(0, count, step):
        both = []
        for h in range(g, g + step, 2):
            value = jnp.where(lane < PITCH, piece(h), piece(h + 1))
            zeroth = value * jnp.where(lane_row < PITCH, is_zeroth(h), is_zeroth(h + 1))
            value = jnp.concatenate([zeroth, value - zeroth], axis=0)
            rest = value - value.astype(jnp.bfloat16).astype(jnp.float32)
            both.append(jnp.concatenate([value, rest], axis=0).astype(jnp.bfloat16))
        both = jnp.concatenate(both, axis=1)
        at = [own(begin + h) for h in range(g, g + step)]
        t_high = jnp.concatenate([high_ref[s] for s in at], axis=0)
        t_low = jnp.concatenate([low_ref[s] for s in at], axis=0)
        total += jnp.dot(both, t_high, preferred_element_type=jnp.float32)
        minor += jnp.dot(both[: 2 * rows], t_low, preferred_element_type=jnp.float32)
    return total[: 2 * rows] + total[2 * rows :] + minor


def first_kernel(part, span, step, meta_ref, v_ref, t_hbm, out_ref, high_hbm, low_hbm, t_ref, high_ref, low_ref, in_sems, out_sems):
    d = pl.program_id(0)
    peers = t_ref.shape[0]
    chunks = in_sems.shape[0]
    each = peers // chunks
    row = lax.broadcasted_iota(jnp.int32, t_ref.shape[1:], 0)

    def fetch(k):
        at = pl.ds(k * each, each)
        return pltpu.make_async_copy(t_hbm.at[at], t_ref.at[at], in_sems.at[k])

    keep_high = pltpu.make_async_copy(high_ref, high_hbm, out_sems.at[0])
    keep_low = pltpu.make_async_copy(low_ref, low_hbm, out_sems.at[1])

    @pl.when(d == 0)
    def _():
        for k in range(chunks):
            fetch(k).start()
        for k in range(chunks):
            fetch(k).wait()

            def split(i, _, k=k):
                s = k * each + i
                value = jnp.where(row < part, t_ref[s], 0.0)
                value = jnp.concatenate([value, jnp.zeros((PITCH - PADDED, value.shape[1]), value.dtype)], axis=0)
                high = value.astype(jnp.bfloat16)
                high_ref[s] = high
                low_ref[s] = (value - high.astype(jnp.float32)).astype(jnp.bfloat16)
                return 0

            lax.fori_loop(0, each, split, 0, unroll=4)
        keep_high.start()
        keep_low.start()

    total = contract(
        part, span, step, meta_ref.shape[1] // 2, lambda i: meta_ref[d, i],
        lambda q: v_ref[0, :, q * LANES : (q + 1) * LANES], v_ref.shape[1], high_ref, low_ref,
    )
    for k in range(out_ref.shape[0]):
        out_ref[k, 0] = total[:, k * LANES : (k + 1) * LANES]

    @pl.when(d == pl.num_programs(0) - 1)
    def _():
        keep_high.wait()
        keep_low.wait()


def first_ladder(meta, got, held, part, span, step):
    cell, rows, width = got.shape
    peers, padded, wide = held.shape
    cores = wide // LANES
    chunks = 8
    anywhere = pl.BlockSpec(memory_space=pl.ANY)
    half = jax.ShapeDtypeStruct((peers, PITCH, wide), jnp.bfloat16)
    return pl.pallas_call(
        functools.partial(first_kernel, part, span, step),
        grid_spec=pltpu.PrefetchScalarGridSpec(
            num_scalar_prefetch=1,
            grid=(cell,),
            in_specs=[pl.BlockSpec((1, rows, width), lambda d, meta: (d, 0, 0)), anywhere],
            out_specs=[pl.BlockSpec((cores, 1, RD * rows, LANES), lambda d, meta: (0, d, 0, 0)), anywhere, anywhere],
            scratch_shapes=[
                pltpu.VMEM((peers, padded, wide), jnp.float32),
                pltpu.VMEM((peers, PITCH, wide), jnp.bfloat16),
                pltpu.VMEM((peers, PITCH, wide), jnp.bfloat16),
                pltpu.SemaphoreType.DMA((chunks,)),
                pltpu.SemaphoreType.DMA((2,)),
            ],
        ),
        out_shape=(jax.ShapeDtypeStruct((cores, cell, RD * rows, LANES), jnp.float32), half, half),
        compiler_params=pltpu.CompilerParams(vmem_limit_bytes=VMEM),
        cost_estimate=pl.CostEstimate(
            flops=12 * RD * rows * cell * span[1] * PITCH * wide, bytes_accessed=4 * got.size + 8 * held.size, transcendentals=0
        ),
    )(meta, got, held)


def last_kernel(part, span, step, meta_ref, core_ref, v_ref, high_ref, low_ref, before_ref, mine_ref, other_ref):
    per = v_ref.shape[0]
    first = pl.program_id(0) * per
    is_first = core_ref[0] == 0

    def block(i, _):
        total = contract(
            part, span, step, meta_ref.shape[1] // 2, lambda k: meta_ref[first + i, k],
            lambda q: v_ref[i, :, q * LANES : (q + 1) * LANES], v_ref.shape[1], high_ref, low_ref,
        )
        lower = before_ref[0, i] + total[:, :LANES]
        upper = before_ref[1, i] + total[:, LANES:]
        mine_ref[i] = jnp.where(is_first, lower, upper)
        other_ref[i] = jnp.where(is_first, upper, lower)
        return 0

    lax.fori_loop(0, per, block, 0)


def last_ladder(meta, core, got, high, low, before, part, span, step):
    cell, rows, width = got.shape
    peers, _, wide = high.shape
    cores = wide // LANES
    per = cell // 2
    whole = pl.BlockSpec((peers, PITCH, wide), lambda d, *_: (0, 0, 0), pipeline_mode=pl.Buffered(1))
    sums = pl.BlockSpec((per, RD * rows, LANES), lambda d, *_: (d, 0, 0))
    shape = jax.ShapeDtypeStruct((cell, RD * rows, LANES), jnp.float32)
    return pl.pallas_call(
        functools.partial(last_kernel, part, span, step),
        grid_spec=pltpu.PrefetchScalarGridSpec(
            num_scalar_prefetch=2,
            grid=(cell // per,),
            in_specs=[
                pl.BlockSpec((per, rows, width), lambda d, *_: (d, 0, 0)),
                whole,
                whole,
                pl.BlockSpec((cores, per, RD * rows, LANES), lambda d, *_: (0, d, 0, 0)),
            ],
            out_specs=[sums, sums],
        ),
        out_shape=(shape, shape),
        compiler_params=pltpu.CompilerParams(vmem_limit_bytes=VMEM),
        cost_estimate=pl.CostEstimate(
            flops=12 * RD * rows * cell * span[1] * PITCH * wide, bytes_accessed=4 * got.size + 4 * high.size, transcendentals=0
        ),
    )(meta, core, got, high, low, before)


def exchange(value, axes):
    return lax.all_to_all(value, axes, split_axis=0, concat_axis=0, tiled=True)


def body(amplitudes, integrals, tile_map, cd_ids, res_ids):
    cell = lax.axis_size(PLANE)
    tiles, rows, depth = integrals.shape
    wide = amplitudes.shape[1]
    part = depth // cell
    peers = tile_map.shape[0]
    shape = tuple(lax.axis_size(a) for a in TILE)
    spans = ((0, FIRST), (FIRST, tiles - FIRST))
    own = exchange(pack(tile_map, cd_ids, res_ids, amplitudes[0].T, cell, shape), PLANE)
    sent, late = cut(integrals, cell, spans)
    ids = own[:, part, : 2 * tiles]
    own, sent, late = lax.optimization_barrier((own, sent, late))
    shared = lax.all_gather(own, "z")
    sent, ids, core = lax.optimization_barrier((sent, ids, lax.axis_index("slab")))
    got = exchange(sent, PLANE)
    got, late, shared, ids, core = lax.optimization_barrier((got, late, shared, ids, core))
    later = exchange(late, PLANE)
    meta = ids.astype(jnp.int32)
    sums, high, low = first_ladder(meta, got, shared.reshape(peers, PADDED, wide), part, spans[0], 8)
    mine, other = last_ladder(meta, core[None], later, high, low, sums, part, spans[1], 8)
    mine += lax.ppermute(other, "slab", [(0, 1), (1, 0)])
    back = exchange(mine, PLANE)
    return jnp.sum(back, axis=0).reshape(RD, rows, LANES)


def solution(mesh):
    grid = Mesh(mesh.devices.reshape(4, 8, 4, 2), TILE + ("slab",))
    placed = (P(TILE, None, "slab"), P(TILE, None, "slab"), P(), P(TILE), P(TILE))
    return jax.shard_map(
        body, mesh=grid, in_specs=placed, out_specs=P(TILE, None, "slab"), check_vma=False
    )
```

```python
import functools

import jax
import jax.numpy as jnp
from jax import lax
from jax.experimental import pallas as pl
from jax.experimental.pallas import tpu as pltpu
from jax.sharding import Mesh, PartitionSpec as P

RD = 2
PLANE = ("y", "x")
TILE = ("y", "z", "x")
LANES = 128
PITCH = 64
PADDED = 56
VMEM = 56 * 1024 * 1024


def pack_kernel(part, tiles, shape, map_ref, cd_ref, res_ref, t_ref, out_ref):
    size_y, size_z, size_x = shape
    square = (LANES, LANES)
    row = lax.broadcasted_iota(jnp.int32, square, 0)
    at_x, at_z, at_y = row % size_x, row // size_x % size_z, row // (size_x * size_z)
    slot = ((at_z * size_y + at_y) * size_x + at_x).astype(jnp.float32)
    ids = jnp.transpose(jnp.broadcast_to(map_ref[...].astype(jnp.float32), square))
    match = ids[:, :tiles] == cd_ref[...].astype(jnp.float32)
    owner = jnp.sum(jnp.where(match, slot[:, :tiles], 0.0), axis=0, keepdims=True)
    ids = jnp.concatenate([owner, res_ref[...].astype(jnp.float32)], axis=1)
    tail = jnp.zeros((PADDED - part, t_ref.shape[1]), jnp.float32)
    for c in range(out_ref.shape[0]):
        out_ref[c, :part, :] = t_ref[c * part : (c + 1) * part, :]
        out_ref[c, part:, :] = tail
        out_ref[c, part : part + 1, : 2 * tiles] = ids


def pack(tile_map, cd_ids, res_ids, turned, cell, shape):
    depth, wide = turned.shape
    part = depth // cell
    tiles = cd_ids.shape[0]
    return pl.pallas_call(
        functools.partial(pack_kernel, part, tiles, shape),
        out_shape=jax.ShapeDtypeStruct((cell, PADDED, wide), jnp.float32),
        compiler_params=pltpu.CompilerParams(vmem_limit_bytes=VMEM),
        cost_estimate=pl.CostEstimate(flops=0, bytes_accessed=depth * wide * 8, transcendentals=0),
    )(tile_map[None], cd_ids[None], res_ids[None], turned)


def cut_kernel(part, v_ref, out_ref):
    depth = v_ref.shape[2]
    lane = lax.broadcasted_iota(jnp.int32, (8, LANES), 1)
    full = depth // LANES

    def source(h, q):
        if q < full:
            return v_ref[h, :, q * LANES : (q + 1) * LANES]
        rest = v_ref[h, :, full * LANES : depth]
        return jnp.concatenate([rest, jnp.zeros((8, LANES - rest.shape[1]), rest.dtype)], axis=1)

    for c in range(out_ref.shape[0]):
        rolled = {}
        for j in range(out_ref.shape[2] // LANES):
            made = None
            at = j * LANES
            while at < (j + 1) * LANES:
                h, v = divmod(at, part)
                q, o = divmod(c * part + v, LANES)
                run = min(part - v, LANES - o, (j + 1) * LANES - at)
                key = (h, q)
                if key not in rolled:
                    shift = (part * (h - c)) % LANES
                    rolled[key] = pltpu.roll(source(h, q), shift, 1) if shift else source(h, q)
                made = rolled[key] if made is None else jnp.where(lane >= at - j * LANES, rolled[key], made)
                at += run
            out_ref[c, :, j * LANES : (j + 1) * LANES] = made


def cut(integrals, cells):
    tiles, rows, depth = integrals.shape
    part = depth // cells
    return pl.pallas_call(
        functools.partial(cut_kernel, part),
        grid=(rows // 8,),
        in_specs=[pl.BlockSpec((tiles, 8, depth), lambda i: (0, i, 0))],
        out_specs=pl.BlockSpec((cells, 8, tiles * part), lambda i: (0, i, 0)),
        out_shape=jax.ShapeDtypeStruct((cells, rows, tiles * part), jnp.float32),
        compiler_params=pltpu.CompilerParams(vmem_limit_bytes=VMEM),
        cost_estimate=pl.CostEstimate(flops=0, bytes_accessed=tiles * rows * depth * 8, transcendentals=0),
    )(integrals)


def ladder_kernel(
    part, step, ids_ref, core_ref, v_hbm, t_hbm, mine_hbm, other_hbm,
    v_ref, t_ref, high_ref, low_ref, mine_ref, other_ref, t_sems, v_sems, mine_sems, other_sems,
):
    peers, _, wide = t_ref.shape
    cell, rows, _ = v_ref.shape
    tiles = v_ref.shape[2] // part
    chunks = t_sems.shape[0]
    ahead = 4
    each = peers // chunks
    lane = lax.broadcasted_iota(jnp.int32, (rows, LANES), 1)
    lane_row = lax.broadcasted_iota(jnp.int32, (1, LANES), 1)
    whole = part // 8 * 8
    row = lax.broadcasted_iota(jnp.int32, (PADDED - whole, wide), 0)

    def fetch_t(k):
        at = pl.ds(k * each, each)
        return pltpu.make_async_copy(t_hbm.at[at], t_ref.at[at], t_sems.at[k])

    def fetch_v(d):
        return pltpu.make_async_copy(v_hbm.at[d], v_ref.at[d], v_sems.at[d])

    def put_mine(d):
        return pltpu.make_async_copy(mine_ref.at[d], mine_hbm.at[d], mine_sems.at[d])

    def put_other(d):
        return pltpu.make_async_copy(other_ref.at[d], other_hbm.at[d], other_sems.at[d])

    for k in range(chunks):
        fetch_t(k).start()
    for d in range(ahead // 2):
        fetch_v(d).start()
    for k in range(chunks):
        fetch_t(k).wait()
        for s in range(k * each, (k + 1) * each):
            ends = jnp.where(row < part - whole, t_ref[s, whole:, :], 0.0)
            pad = jnp.zeros((PITCH - PADDED, wide), jnp.float32)
            value = jnp.concatenate([t_ref[s, :whole, :], ends, pad], axis=0)
            high = value.astype(jnp.bfloat16)
            high_ref[s] = high
            low_ref[s] = (value - high.astype(jnp.float32)).astype(jnp.bfloat16)

    for d in range(ahead // 2, ahead):
        fetch_v(d).start()
    is_first = core_ref[0] == 0

    def block(d, _):
        @pl.when(d + ahead < cell)
        def _():
            fetch_v(d + ahead).start()

        fetch_v(d).wait()
        total = contract(d)
        mine_ref[d] = jnp.where(is_first, total[:, :LANES], total[:, LANES:])
        other_ref[d] = jnp.where(is_first, total[:, LANES:], total[:, :LANES])
        put_mine(d).start()
        put_other(d).start()
        return 0

    def contract(d):
        def load(q):
            return v_ref[d, :, q * LANES : (q + 1) * LANES]

        def piece(h):
            q, o = divmod(part * h, LANES)
            base = PITCH * (h % 2)
            shift = (base - o) % LANES
            first = pltpu.roll(load(q), shift, 1) if shift else load(q)
            if o + part <= LANES:
                return first
            second = pltpu.roll(load(q + 1), shift, 1) if shift else load(q + 1)
            return jnp.where(lane < base + LANES - o, first, second)

        total = jnp.zeros((4 * rows, wide), jnp.float32)
        minor = jnp.zeros((2 * rows, wide), jnp.float32)
        for g in range(0, tiles, step):
            both = []
            for h in range(g, g + step, 2):
                value = jnp.where(lane < PITCH, piece(h), piece(h + 1))
                zeroth = value * (1.0 - jnp.where(lane_row < PITCH, ids_ref[d, tiles + h], ids_ref[d, tiles + h + 1]))
                value = jnp.concatenate([zeroth, value - zeroth], axis=0)
                rest = value - value.astype(jnp.bfloat16).astype(jnp.float32)
                both.append(jnp.concatenate([value, rest], axis=0).astype(jnp.bfloat16))
            both = jnp.concatenate(both, axis=1)
            at = [ids_ref[d, h].astype(jnp.int32) for h in range(g, g + step)]
            t_high = jnp.concatenate([high_ref[s] for s in at], axis=0)
            t_low = jnp.concatenate([low_ref[s] for s in at], axis=0)
            total += jnp.dot(both, t_high, preferred_element_type=jnp.float32)
            minor += jnp.dot(both[: 2 * rows], t_low, preferred_element_type=jnp.float32)
        return total[: 2 * rows] + total[2 * rows :] + minor

    lax.fori_loop(0, cell, block, 0)
    for d in range(cell):
        put_mine(d).wait()
        put_other(d).wait()


def ladder(ids, core, got, held, part, step):
    cell, rows, width = got.shape
    peers, padded, wide = held.shape
    chunks = 8
    anywhere = pl.BlockSpec(memory_space=pl.ANY)
    scalars = pl.BlockSpec(memory_space=pltpu.SMEM)
    shape = jax.ShapeDtypeStruct((cell, RD * rows, LANES), jnp.float32)
    return pl.pallas_call(
        functools.partial(ladder_kernel, part, step),
        in_specs=[scalars, scalars, anywhere, anywhere],
        out_specs=[anywhere, anywhere],
        out_shape=(shape, shape),
        scratch_shapes=[
            pltpu.VMEM((cell, rows, width), jnp.float32),
            pltpu.VMEM((peers, padded, wide), jnp.float32),
            pltpu.VMEM((peers, PITCH, wide), jnp.bfloat16),
            pltpu.VMEM((peers, PITCH, wide), jnp.bfloat16),
            pltpu.VMEM(shape.shape, jnp.float32),
            pltpu.VMEM(shape.shape, jnp.float32),
            pltpu.SemaphoreType.DMA((chunks,)),
            pltpu.SemaphoreType.DMA((cell,)),
            pltpu.SemaphoreType.DMA((cell,)),
            pltpu.SemaphoreType.DMA((cell,)),
        ],
        compiler_params=pltpu.CompilerParams(vmem_limit_bytes=VMEM),
        cost_estimate=pl.CostEstimate(
            flops=12 * rows * got.size // rows * PITCH // part * wide * RD, bytes_accessed=4 * (got.size + held.size), transcendentals=0
        ),
    )(ids, core, got, held)


def exchange(value, axes):
    return lax.all_to_all(value, axes, split_axis=0, concat_axis=0, tiled=True)


def body(amplitudes, integrals, tile_map, cd_ids, res_ids):
    cell = lax.axis_size(PLANE)
    tiles, rows, depth = integrals.shape
    wide = amplitudes.shape[1]
    part = depth // cell
    peers = tile_map.shape[0]
    shape = tuple(lax.axis_size(a) for a in TILE)
    own = exchange(pack(tile_map, cd_ids, res_ids, amplitudes[0].T, cell, shape), PLANE)
    sent = cut(integrals, cell)
    ids = own[:, part, : 2 * tiles]
    own, sent = lax.optimization_barrier((own, sent))
    shared = lax.all_gather(own, "z").reshape(peers, PADDED, wide)
    sent, ids, core = lax.optimization_barrier((sent, ids, lax.axis_index("slab")))
    got = exchange(sent, PLANE)
    got, shared, ids, core = lax.optimization_barrier((got, shared, ids, core))
    mine, other = ladder(ids, core[None], got, shared, part, 16)
    mine += lax.ppermute(other, "slab", [(0, 1), (1, 0)])
    back = exchange(mine, PLANE)
    return jnp.sum(back, axis=0).reshape(RD, rows, LANES)


def solution(mesh):
    grid = Mesh(mesh.devices.reshape(4, 8, 4, 2), TILE + ("slab",))
    placed = (P(TILE, None, "slab"), P(TILE, None, "slab"), P(), P(TILE), P(TILE))
    return jax.shard_map(
        body, mesh=grid, in_specs=placed, out_specs=P(TILE, None, "slab"), check_vma=False
    )
```

```python
import functools

import jax
import jax.numpy as jnp
from jax import lax
from jax.experimental import pallas as pl
from jax.experimental.pallas import tpu as pltpu
from jax.sharding import Mesh, PartitionSpec as P

RD = 2
PLANE = ("y", "x")
TILE = ("y", "z", "x")
LANES = 128
PITCH = 64
PADDED = 56
VMEM = 56 * 1024 * 1024


def pack_kernel(part, tiles, shape, map_ref, cd_ref, res_ref, t_hbm, out_hbm, t_ref, out_ref, in_sems, out_sems):
    size_y, size_z, size_x = shape
    cells = out_ref.shape[0]
    pieces = in_sems.shape[0]
    each = cells // pieces

    def fetch(k):
        at = pl.ds(k * each * part, each * part)
        return pltpu.make_async_copy(t_hbm.at[at], t_ref.at[at], in_sems.at[k])

    def put(k):
        at = pl.ds(k * each, each)
        return pltpu.make_async_copy(out_ref.at[at], out_hbm.at[at], out_sems.at[k])

    for k in range(pieces):
        fetch(k).start()
    square = (LANES, LANES)
    row = lax.broadcasted_iota(jnp.int32, square, 0)
    at_x, at_z, at_y = row % size_x, row // size_x % size_z, row // (size_x * size_z)
    slot = ((at_z * size_y + at_y) * size_x + at_x).astype(jnp.float32)
    ids = jnp.transpose(jnp.broadcast_to(map_ref[...].astype(jnp.float32), square))
    match = ids[:, :tiles] == cd_ref[...].astype(jnp.float32)
    owner = jnp.sum(jnp.where(match, slot[:, :tiles], 0.0), axis=0, keepdims=True)
    ids = jnp.concatenate([owner, res_ref[...].astype(jnp.float32)], axis=1)
    tail = jnp.zeros((PADDED - part, t_ref.shape[1]), jnp.float32)
    for k in range(pieces):
        fetch(k).wait()
        for c in range(k * each, (k + 1) * each):
            out_ref[c, :part, :] = t_ref[c * part : (c + 1) * part, :]
            out_ref[c, part:, :] = tail
            out_ref[c, part : part + 1, : 2 * tiles] = ids
        put(k).start()
    for k in range(pieces):
        put(k).wait()


def pack(tile_map, cd_ids, res_ids, turned, cell, shape):
    depth, wide = turned.shape
    part = depth // cell
    tiles = cd_ids.shape[0]
    pieces = 4
    small = pl.BlockSpec(memory_space=pltpu.VMEM)
    anywhere = pl.BlockSpec(memory_space=pl.ANY)
    return pl.pallas_call(
        functools.partial(pack_kernel, part, tiles, shape),
        in_specs=[small, small, small, anywhere],
        out_specs=anywhere,
        out_shape=jax.ShapeDtypeStruct((cell, PADDED, wide), jnp.float32),
        scratch_shapes=[
            pltpu.VMEM((depth, wide), jnp.float32),
            pltpu.VMEM((cell, PADDED, wide), jnp.float32),
            pltpu.SemaphoreType.DMA((pieces,)),
            pltpu.SemaphoreType.DMA((pieces,)),
        ],
        compiler_params=pltpu.CompilerParams(vmem_limit_bytes=VMEM),
        cost_estimate=pl.CostEstimate(flops=0, bytes_accessed=depth * wide * 8, transcendentals=0),
    )(tile_map[None], cd_ids[None], res_ids[None], turned)


def cut_kernel(part, v_ref, out_ref):
    depth = v_ref.shape[2]
    lane = lax.broadcasted_iota(jnp.int32, (8, LANES), 1)
    full = depth // LANES

    def source(h, q):
        if q < full:
            return v_ref[h, :, q * LANES : (q + 1) * LANES]
        rest = v_ref[h, :, full * LANES : depth]
        return jnp.concatenate([rest, jnp.zeros((8, LANES - rest.shape[1]), rest.dtype)], axis=1)

    for c in range(out_ref.shape[0]):
        rolled = {}
        for j in range(out_ref.shape[2] // LANES):
            made = None
            at = j * LANES
            while at < (j + 1) * LANES:
                h, v = divmod(at, part)
                q, o = divmod(c * part + v, LANES)
                run = min(part - v, LANES - o, (j + 1) * LANES - at)
                key = (h, q)
                if key not in rolled:
                    shift = (part * (h - c)) % LANES
                    rolled[key] = pltpu.roll(source(h, q), shift, 1) if shift else source(h, q)
                made = rolled[key] if made is None else jnp.where(lane >= at - j * LANES, rolled[key], made)
                at += run
            out_ref[c, :, j * LANES : (j + 1) * LANES] = made


def cut(integrals, cells):
    tiles, rows, depth = integrals.shape
    part = depth // cells
    return pl.pallas_call(
        functools.partial(cut_kernel, part),
        grid=(rows // 8,),
        in_specs=[pl.BlockSpec((tiles, 8, depth), lambda i: (0, i, 0))],
        out_specs=pl.BlockSpec((cells, 8, tiles * part), lambda i: (0, i, 0)),
        out_shape=jax.ShapeDtypeStruct((cells, rows, tiles * part), jnp.float32),
        compiler_params=pltpu.CompilerParams(vmem_limit_bytes=VMEM),
        cost_estimate=pl.CostEstimate(flops=0, bytes_accessed=tiles * rows * depth * 8, transcendentals=0),
    )(integrals)


def ladder_kernel(
    part, step, at_ref, v_hbm, t_hbm, mine_hbm, other_hbm,
    v_ref, t_ref, high_ref, low_ref, mine_ref, other_ref, ids_ref, t_sems, v_sems, mine_sems, other_sems, ids_sem,
):
    peers, _, wide = t_ref.shape
    cell, rows, _ = v_ref.shape
    tiles = v_ref.shape[2] // part
    chunks = t_sems.shape[0]
    ahead = 4
    each = peers // chunks
    lane = lax.broadcasted_iota(jnp.int32, (rows, LANES), 1)
    lane_row = lax.broadcasted_iota(jnp.int32, (1, LANES), 1)
    whole = part // 8 * 8
    row = lax.broadcasted_iota(jnp.int32, (PADDED - whole, wide), 0)

    def fetch_t(k):
        at = pl.ds(k * each, each)
        return pltpu.make_async_copy(t_hbm.at[at], t_ref.at[at], t_sems.at[k])

    def fetch_v(d):
        return pltpu.make_async_copy(v_hbm.at[d], v_ref.at[d], v_sems.at[d])

    def put_mine(d):
        return pltpu.make_async_copy(mine_ref.at[d], mine_hbm.at[d], mine_sems.at[d])

    def put_other(d):
        return pltpu.make_async_copy(other_ref.at[d], other_hbm.at[d], other_sems.at[d])

    def own(d, i):
        return ids_ref[d, part - whole, i]

    fetch_ids = pltpu.make_async_copy(
        t_hbm.at[pl.ds(at_ref[1] * cell, cell), pl.ds(whole, 8), pl.ds(0, LANES)], ids_ref, ids_sem
    )
    fetch_ids.start()
    for k in range(chunks):
        fetch_t(k).start()
    for d in range(ahead // 2):
        fetch_v(d).start()
    for k in range(chunks):
        fetch_t(k).wait()
        for s in range(k * each, (k + 1) * each):
            ends = jnp.where(row < part - whole, t_ref[s, whole:, :], 0.0)
            pad = jnp.zeros((PITCH - PADDED, wide), jnp.float32)
            value = jnp.concatenate([t_ref[s, :whole, :], ends, pad], axis=0)
            high = value.astype(jnp.bfloat16)
            high_ref[s] = high
            low_ref[s] = (value - high.astype(jnp.float32)).astype(jnp.bfloat16)

    for d in range(ahead // 2, ahead):
        fetch_v(d).start()
    fetch_ids.wait()
    is_first = at_ref[0] == 0

    def block(d, _):
        @pl.when(d + ahead < cell)
        def _():
            fetch_v(d + ahead).start()

        fetch_v(d).wait()
        total = contract(d)
        mine_ref[d] = jnp.where(is_first, total[:, :LANES], total[:, LANES:])
        other_ref[d] = jnp.where(is_first, total[:, LANES:], total[:, :LANES])
        put_mine(d).start()
        put_other(d).start()
        return 0

    def contract(d):
        def load(q):
            return v_ref[d, :, q * LANES : (q + 1) * LANES]

        def piece(h):
            q, o = divmod(part * h, LANES)
            base = PITCH * (h % 2)
            shift = (base - o) % LANES
            first = pltpu.roll(load(q), shift, 1) if shift else load(q)
            if o + part <= LANES:
                return first
            second = pltpu.roll(load(q + 1), shift, 1) if shift else load(q + 1)
            return jnp.where(lane < base + LANES - o, first, second)

        total = jnp.zeros((4 * rows, wide), jnp.float32)
        minor = jnp.zeros((2 * rows, wide), jnp.float32)
        for g in range(0, tiles, step):
            both = []
            for h in range(g, g + step, 2):
                value = jnp.where(lane < PITCH, piece(h), piece(h + 1))
                zeroth = value * (1.0 - jnp.where(lane_row < PITCH, own(d, tiles + h), own(d, tiles + h + 1)))
                value = jnp.concatenate([zeroth, value - zeroth], axis=0)
                rest = value - value.astype(jnp.bfloat16).astype(jnp.float32)
                both.append(jnp.concatenate([value, rest], axis=0).astype(jnp.bfloat16))
            both = jnp.concatenate(both, axis=1)
            at = [own(d, h).astype(jnp.int32) for h in range(g, g + step)]
            t_high = jnp.concatenate([high_ref[s] for s in at], axis=0)
            t_low = jnp.concatenate([low_ref[s] for s in at], axis=0)
            total += jnp.dot(both, t_high, preferred_element_type=jnp.float32)
            minor += jnp.dot(both[: 2 * rows], t_low, preferred_element_type=jnp.float32)
        return total[: 2 * rows] + total[2 * rows :] + minor

    lax.fori_loop(0, cell, block, 0)
    for d in range(cell):
        put_mine(d).wait()
        put_other(d).wait()


def ladder(at, got, held, part, step):
    cell, rows, width = got.shape
    peers, padded, wide = held.shape
    chunks = 8
    anywhere = pl.BlockSpec(memory_space=pl.ANY)
    shape = jax.ShapeDtypeStruct((cell, RD * rows, LANES), jnp.float32)
    return pl.pallas_call(
        functools.partial(ladder_kernel, part, step),
        in_specs=[pl.BlockSpec(memory_space=pltpu.SMEM), anywhere, anywhere],
        out_specs=[anywhere, anywhere],
        out_shape=(shape, shape),
        scratch_shapes=[
            pltpu.VMEM((cell, rows, width), jnp.float32),
            pltpu.VMEM((peers, padded, wide), jnp.float32),
            pltpu.VMEM((peers, PITCH, wide), jnp.bfloat16),
            pltpu.VMEM((peers, PITCH, wide), jnp.bfloat16),
            pltpu.VMEM(shape.shape, jnp.float32),
            pltpu.VMEM(shape.shape, jnp.float32),
            pltpu.SMEM((cell, 8, LANES), jnp.float32),
            pltpu.SemaphoreType.DMA((chunks,)),
            pltpu.SemaphoreType.DMA((cell,)),
            pltpu.SemaphoreType.DMA((cell,)),
            pltpu.SemaphoreType.DMA((cell,)),
            pltpu.SemaphoreType.DMA,
        ],
        compiler_params=pltpu.CompilerParams(vmem_limit_bytes=VMEM),
        cost_estimate=pl.CostEstimate(
            flops=12 * rows * got.size // rows * PITCH // part * wide * RD, bytes_accessed=4 * (got.size + held.size), transcendentals=0
        ),
    )(at, got, held)


def exchange(value, axes):
    return lax.all_to_all(value, axes, split_axis=0, concat_axis=0, tiled=True)


def body(amplitudes, integrals, tile_map, cd_ids, res_ids):
    cell = lax.axis_size(PLANE)
    tiles, rows, depth = integrals.shape
    wide = amplitudes.shape[1]
    part = depth // cell
    peers = tile_map.shape[0]
    shape = tuple(lax.axis_size(a) for a in TILE)
    own = exchange(pack(tile_map, cd_ids, res_ids, amplitudes[0].T, cell, shape), PLANE)
    sent = cut(integrals, cell)
    own, sent = lax.optimization_barrier((own, sent))
    shared = lax.all_gather(own, "z").reshape(peers, PADDED, wide)
    at = jnp.stack([lax.axis_index("slab"), lax.axis_index("z")])
    sent, at = lax.optimization_barrier((sent, at))
    got = exchange(sent, PLANE)
    got, shared, at = lax.optimization_barrier((got, shared, at))
    mine, other = ladder(at, got, shared, part, 16)
    mine += lax.ppermute(other, "slab", [(0, 1), (1, 0)])
    back = exchange(mine, PLANE)
    return jnp.sum(back, axis=0).reshape(RD, rows, LANES)


def solution(mesh):
    grid = Mesh(mesh.devices.reshape(4, 8, 4, 2), TILE + ("slab",))
    placed = (P(TILE, None, "slab"), P(TILE, None, "slab"), P(), P(TILE), P(TILE))
    return jax.shard_map(
        body, mesh=grid, in_specs=placed, out_specs=P(TILE, None, "slab"), check_vma=False
    )
```

```python
import functools

import jax
import jax.numpy as jnp
from jax import lax
from jax.experimental import pallas as pl
from jax.experimental.pallas import tpu as pltpu
from jax.sharding import Mesh, PartitionSpec as P

RD = 2
PLANE = ("y", "x")
TILE = ("y", "z", "x")
LANES = 128
PITCH = 64
PADDED = 56
VMEM = 56 * 1024 * 1024
CUT_VMEM = (64 * 1024 - 512) * 1024


def pack_kernel(part, tiles, shape, map_ref, cd_ref, res_ref, t_ref, out_ref):
    size_y, size_z, size_x = shape
    square = (LANES, LANES)
    row = lax.broadcasted_iota(jnp.int32, square, 0)
    at_x, at_z, at_y = row % size_x, row // size_x % size_z, row // (size_x * size_z)
    slot = ((at_z * size_y + at_y) * size_x + at_x).astype(jnp.float32)
    ids = jnp.transpose(jnp.broadcast_to(map_ref[...].astype(jnp.float32), square))
    match = ids[:, :tiles] == cd_ref[...].astype(jnp.float32)
    owner = jnp.sum(jnp.where(match, slot[:, :tiles], 0.0), axis=0, keepdims=True)
    ids = jnp.concatenate([owner, res_ref[...].astype(jnp.float32)], axis=1)
    tail = jnp.zeros((PADDED - part, t_ref.shape[1]), jnp.float32)
    for c in range(out_ref.shape[0]):
        out_ref[c, :part, :] = t_ref[c * part : (c + 1) * part, :]
        out_ref[c, part:, :] = tail
        out_ref[c, part : part + 1, : 2 * tiles] = ids


def pack(tile_map, cd_ids, res_ids, turned, cell, shape):
    depth, wide = turned.shape
    part = depth // cell
    tiles = cd_ids.shape[0]
    return pl.pallas_call(
        functools.partial(pack_kernel, part, tiles, shape),
        out_shape=jax.ShapeDtypeStruct((cell, PADDED, wide), jnp.float32),
        compiler_params=pltpu.CompilerParams(vmem_limit_bytes=VMEM),
        cost_estimate=pl.CostEstimate(flops=0, bytes_accessed=depth * wide * 8, transcendentals=0),
    )(tile_map[None], cd_ids[None], res_ids[None], turned)


def cut_kernel(part, v_ref, out_ref):
    depth = v_ref.shape[2]
    lane = lax.broadcasted_iota(jnp.int32, (8, LANES), 1)
    full = depth // LANES

    def source(h, q):
        if q < full:
            return v_ref[h, :, q * LANES : (q + 1) * LANES]
        rest = v_ref[h, :, full * LANES : depth]
        return jnp.concatenate([rest, jnp.zeros((8, LANES - rest.shape[1]), rest.dtype)], axis=1)

    for c in range(out_ref.shape[0]):
        rolled = {}
        for j in range(out_ref.shape[2] // LANES):
            made = None
            at = j * LANES
            while at < (j + 1) * LANES:
                h, v = divmod(at, part)
                q, o = divmod(c * part + v, LANES)
                run = min(part - v, LANES - o, (j + 1) * LANES - at)
                key = (h, q)
                if key not in rolled:
                    shift = (part * (h - c)) % LANES
                    rolled[key] = pltpu.roll(source(h, q), shift, 1) if shift else source(h, q)
                made = rolled[key] if made is None else jnp.where(lane >= at - j * LANES, rolled[key], made)
                at += run
            out_ref[c, :, j * LANES : (j + 1) * LANES] = made


def cut(integrals, cells):
    tiles, rows, depth = integrals.shape
    part = depth // cells
    return pl.pallas_call(
        functools.partial(cut_kernel, part),
        grid=(rows // 8,),
        in_specs=[pl.BlockSpec((tiles, 8, depth), lambda i: (0, i, 0))],
        out_specs=pl.BlockSpec((cells, 8, tiles * part), lambda i: (0, i, 0)),
        out_shape=jax.ShapeDtypeStruct((cells, rows, tiles * part), jnp.float32),
        compiler_params=pltpu.CompilerParams(vmem_limit_bytes=CUT_VMEM),
        cost_estimate=pl.CostEstimate(flops=0, bytes_accessed=tiles * rows * depth * 8, transcendentals=0),
    )(integrals)


def ladder_kernel(
    part, step, core_ref, plane_ref, v_hbm, t_hbm, mine_hbm, other_hbm,
    v_ref, t_ref, high_ref, low_ref, mine_ref, other_ref, ids_ref, t_sems, v_sems, mine_sems, other_sems, ids_sem,
):
    peers, _, wide = t_ref.shape
    cell, rows, _ = v_ref.shape
    tiles = v_ref.shape[2] // part
    chunks = t_sems.shape[0]
    ahead = 4
    each = peers // chunks
    lane = lax.broadcasted_iota(jnp.int32, (rows, LANES), 1)
    lane_row = lax.broadcasted_iota(jnp.int32, (1, LANES), 1)
    whole = part // 8 * 8
    row = lax.broadcasted_iota(jnp.int32, (PADDED - whole, wide), 0)

    def fetch_t(k):
        at = pl.ds(k * each, each)
        return pltpu.make_async_copy(t_hbm.at[at], t_ref.at[at], t_sems.at[k])

    def fetch_v(d):
        return pltpu.make_async_copy(v_hbm.at[d], v_ref.at[d], v_sems.at[d])

    def put_mine(d):
        return pltpu.make_async_copy(mine_ref.at[d], mine_hbm.at[d], mine_sems.at[d])

    def put_other(d):
        return pltpu.make_async_copy(other_ref.at[d], other_hbm.at[d], other_sems.at[d])

    def own(d, i):
        return ids_ref[d, part - whole, i]

    fetch_ids = pltpu.make_async_copy(
        t_hbm.at[pl.ds(plane_ref[0] * cell, cell), pl.ds(whole, 8), pl.ds(0, LANES)], ids_ref, ids_sem
    )
    fetch_ids.start()
    for k in range(chunks):
        fetch_t(k).start()
    for d in range(ahead // 2):
        fetch_v(d).start()
    for k in range(chunks):
        fetch_t(k).wait()
        for s in range(k * each, (k + 1) * each):
            ends = jnp.where(row < part - whole, t_ref[s, whole:, :], 0.0)
            pad = jnp.zeros((PITCH - PADDED, wide), jnp.float32)
            value = jnp.concatenate([t_ref[s, :whole, :], ends, pad], axis=0)
            high = value.astype(jnp.bfloat16)
            high_ref[s] = high
            low_ref[s] = (value - high.astype(jnp.float32)).astype(jnp.bfloat16)

    for d in range(ahead // 2, ahead):
        fetch_v(d).start()
    fetch_ids.wait()
    is_first = core_ref[0] == 0

    def block(d, _):
        @pl.when(d + ahead < cell)
        def _():
            fetch_v(d + ahead).start()

        fetch_v(d).wait()
        total = contract(d)
        mine_ref[d] = jnp.where(is_first, total[:, :LANES], total[:, LANES:])
        other_ref[d] = jnp.where(is_first, total[:, LANES:], total[:, :LANES])
        put_mine(d).start()
        put_other(d).start()
        return 0

    def contract(d):
        def load(q):
            return v_ref[d, :, q * LANES : (q + 1) * LANES]

        def piece(h):
            q, o = divmod(part * h, LANES)
            base = PITCH * (h % 2)
            shift = (base - o) % LANES
            first = pltpu.roll(load(q), shift, 1) if shift else load(q)
            if o + part <= LANES:
                return first
            second = pltpu.roll(load(q + 1), shift, 1) if shift else load(q + 1)
            return jnp.where(lane < base + LANES - o, first, second)

        total = jnp.zeros((4 * rows, wide), jnp.float32)
        minor = jnp.zeros((2 * rows, wide), jnp.float32)
        for g in range(0, tiles, step):
            both = []
            for h in range(g, g + step, 2):
                value = jnp.where(lane < PITCH, piece(h), piece(h + 1))
                zeroth = value * (1.0 - jnp.where(lane_row < PITCH, own(d, tiles + h), own(d, tiles + h + 1)))
                value = jnp.concatenate([zeroth, value - zeroth], axis=0)
                rest = value - value.astype(jnp.bfloat16).astype(jnp.float32)
                both.append(jnp.concatenate([value, rest], axis=0).astype(jnp.bfloat16))
            both = jnp.concatenate(both, axis=1)
            at = [own(d, h).astype(jnp.int32) for h in range(g, g + step)]
            t_high = jnp.concatenate([high_ref[s] for s in at], axis=0)
            t_low = jnp.concatenate([low_ref[s] for s in at], axis=0)
            total += jnp.dot(both, t_high, preferred_element_type=jnp.float32)
            minor += jnp.dot(both[: 2 * rows], t_low, preferred_element_type=jnp.float32)
        return total[: 2 * rows] + total[2 * rows :] + minor

    lax.fori_loop(0, cell, block, 0)
    for d in range(cell):
        put_mine(d).wait()
        put_other(d).wait()


def ladder(core, plane, got, held, part, step):
    cell, rows, width = got.shape
    peers, padded, wide = held.shape
    chunks = 8
    anywhere = pl.BlockSpec(memory_space=pl.ANY)
    scalar = pl.BlockSpec(memory_space=pltpu.SMEM)
    shape = jax.ShapeDtypeStruct((cell, RD * rows, LANES), jnp.float32)
    return pl.pallas_call(
        functools.partial(ladder_kernel, part, step),
        in_specs=[scalar, scalar, anywhere, anywhere],
        out_specs=[anywhere, anywhere],
        out_shape=(shape, shape),
        scratch_shapes=[
            pltpu.VMEM((cell, rows, width), jnp.float32),
            pltpu.VMEM((peers, padded, wide), jnp.float32),
            pltpu.VMEM((peers, PITCH, wide), jnp.bfloat16),
            pltpu.VMEM((peers, PITCH, wide), jnp.bfloat16),
            pltpu.VMEM(shape.shape, jnp.float32),
            pltpu.VMEM(shape.shape, jnp.float32),
            pltpu.SMEM((cell, 8, LANES), jnp.float32),
            pltpu.SemaphoreType.DMA((chunks,)),
            pltpu.SemaphoreType.DMA((cell,)),
            pltpu.SemaphoreType.DMA((cell,)),
            pltpu.SemaphoreType.DMA((cell,)),
            pltpu.SemaphoreType.DMA,
        ],
        compiler_params=pltpu.CompilerParams(vmem_limit_bytes=VMEM),
        cost_estimate=pl.CostEstimate(
            flops=12 * rows * got.size // rows * PITCH // part * wide * RD, bytes_accessed=4 * (got.size + held.size), transcendentals=0
        ),
    )(core, plane, got, held)


def exchange(value, axes):
    return lax.all_to_all(value, axes, split_axis=0, concat_axis=0, tiled=True)


def body(amplitudes, integrals, tile_map, cd_ids, res_ids):
    cell = lax.axis_size(PLANE)
    tiles, rows, depth = integrals.shape
    wide = amplitudes.shape[1]
    part = depth // cell
    peers = tile_map.shape[0]
    shape = tuple(lax.axis_size(a) for a in TILE)
    own = exchange(pack(tile_map, cd_ids, res_ids, amplitudes[0].T, cell, shape), PLANE)
    sent = cut(integrals, cell)
    own, sent = lax.optimization_barrier((own, sent))
    shared = lax.all_gather(own, "z").reshape(peers, PADDED, wide)
    sent, core, plane = lax.optimization_barrier((sent, lax.axis_index("slab"), lax.axis_index("z")))
    got = exchange(sent, PLANE)
    got, shared, core, plane = lax.optimization_barrier((got, shared, core, plane))
    mine, other = ladder(core[None], plane[None], got, shared, part, 16)
    mine += lax.ppermute(other, "slab", [(0, 1), (1, 0)])
    back = exchange(mine, PLANE)
    return jnp.sum(back, axis=0).reshape(RD, rows, LANES)


def solution(mesh):
    grid = Mesh(mesh.devices.reshape(4, 8, 4, 2), TILE + ("slab",))
    placed = (P(TILE, None, "slab"), P(TILE, None, "slab"), P(), P(TILE), P(TILE))
    return jax.shard_map(
        body, mesh=grid, in_specs=placed, out_specs=P(TILE, None, "slab"), check_vma=False
    )
```

```python
import functools

import jax
import jax.numpy as jnp
from jax import lax
from jax.experimental import pallas as pl
from jax.experimental.pallas import tpu as pltpu
from jax.sharding import Mesh, PartitionSpec as P

RD = 2
PLANE = ("y", "x")
TILE = ("y", "z", "x")
LANES = 128
MAIN = 48
PADDED = 56
VMEM = 56 * 1024 * 1024
CUT_VMEM = (64 * 1024 - 512) * 1024


def pack_kernel(part, tiles, shape, map_ref, cd_ref, res_ref, t_ref, out_ref):
    size_y, size_z, size_x = shape
    square = (LANES, LANES)
    row = lax.broadcasted_iota(jnp.int32, square, 0)
    at_x, at_z, at_y = row % size_x, row // size_x % size_z, row // (size_x * size_z)
    slot = ((at_z * size_y + at_y) * size_x + at_x).astype(jnp.float32)
    ids = jnp.transpose(jnp.broadcast_to(map_ref[...].astype(jnp.float32), square))
    match = ids[:, :tiles] == cd_ref[...].astype(jnp.float32)
    owner = jnp.sum(jnp.where(match, slot[:, :tiles], 0.0), axis=0, keepdims=True)
    target = res_ref[...].astype(jnp.float32)
    ids = jnp.concatenate([owner, target], axis=1)
    row, lane = row[:tiles], lax.broadcasted_iota(jnp.int32, (tiles, LANES), 1)
    pairs = (lane // 2 == row).astype(jnp.float32)
    down = jnp.transpose(jnp.broadcast_to(ids, square))
    owners = jnp.sum(pairs * down[:tiles], axis=0, keepdims=True)
    targets = jnp.sum(pairs * down[tiles:], axis=0, keepdims=True)
    tail = jnp.zeros((PADDED - part, t_ref.shape[1]), jnp.float32)
    for c in range(out_ref.shape[0]):
        out_ref[c, :part, :] = t_ref[c * part : (c + 1) * part, :]
        out_ref[c, part:, :] = tail
        out_ref[c, part : part + 1, : 2 * tiles] = ids
        out_ref[c, part + 1 : part + 2, :LANES] = owners
        out_ref[c, part + 2 : part + 3, :LANES] = targets


def pack(tile_map, cd_ids, res_ids, turned, cell, shape):
    depth, wide = turned.shape
    part = depth // cell
    tiles = cd_ids.shape[0]
    return pl.pallas_call(
        functools.partial(pack_kernel, part, tiles, shape),
        out_shape=jax.ShapeDtypeStruct((cell, PADDED, wide), jnp.float32),
        compiler_params=pltpu.CompilerParams(vmem_limit_bytes=VMEM),
        cost_estimate=pl.CostEstimate(flops=0, bytes_accessed=depth * wide * 8, transcendentals=0),
    )(tile_map[None], cd_ids[None], res_ids[None], turned)


def cut_kernel(part, v_ref, out_ref):
    tiles, _, depth = v_ref.shape
    lane = lax.broadcasted_iota(jnp.int32, (8, LANES), 1)
    full = depth // LANES

    def source(h, q):
        if q < full:
            return v_ref[h, :, q * LANES : (q + 1) * LANES]
        rest = v_ref[h, :, full * LANES : depth]
        return jnp.concatenate([rest, jnp.zeros((8, LANES - rest.shape[1]), rest.dtype)], axis=1)

    for c in range(out_ref.shape[0]):
        rolled = {}
        for j in range(out_ref.shape[2] // LANES):
            made = None
            at = j * LANES
            while at < (j + 1) * LANES:
                h, v = divmod(at, MAIN) if at < MAIN * tiles else divmod(at - MAIN * tiles, part - MAIN)
                length = MAIN if at < MAIN * tiles else part - MAIN
                left = 0 if at < MAIN * tiles else MAIN
                q, o = divmod(c * part + left + v, LANES)
                run = min(length - v, LANES - o, (j + 1) * LANES - at)
                key = (h, q, left)
                if key not in rolled:
                    shift = (at - o) % LANES
                    rolled[key] = pltpu.roll(source(h, q), shift, 1) if shift else source(h, q)
                made = rolled[key] if made is None else jnp.where(lane >= at - j * LANES, rolled[key], made)
                at += run
            out_ref[c, :, j * LANES : (j + 1) * LANES] = made


def cut(integrals, cells):
    tiles, rows, depth = integrals.shape
    part = depth // cells
    return pl.pallas_call(
        functools.partial(cut_kernel, part),
        grid=(rows // 8,),
        in_specs=[pl.BlockSpec((tiles, 8, depth), lambda i: (0, i, 0))],
        out_specs=pl.BlockSpec((cells, 8, tiles * part), lambda i: (0, i, 0)),
        out_shape=jax.ShapeDtypeStruct((cells, rows, tiles * part), jnp.float32),
        compiler_params=pltpu.CompilerParams(vmem_limit_bytes=CUT_VMEM),
        cost_estimate=pl.CostEstimate(flops=0, bytes_accessed=tiles * rows * depth * 8, transcendentals=0),
    )(integrals)


def ladder_kernel(
    part, step, core_ref, plane_ref, v_hbm, t_hbm, mine_hbm, other_hbm,
    v_ref, t_ref, high_ref, low_ref, rest_ref, pairs_ref, few_ref, routed_ref, start_ref, mine_ref, other_ref, ids_ref,
    t_sems, v_sems, mine_sems, other_sems, ids_sem, pairs_sem, few_sem,
):
    peers, _, wide = t_ref.shape
    cell, rows, _ = v_ref.shape
    tiles = v_ref.shape[2] // part
    chunks = t_sems.shape[0]
    ahead = 4
    each = peers // chunks
    lane_row = lax.broadcasted_iota(jnp.int32, (1, LANES), 1)
    few = part - MAIN
    place = lax.broadcasted_iota(jnp.int32, (LANES, few * peers), 1)
    which = lax.broadcasted_iota(jnp.int32, (LANES, few * peers), 0) % few

    def fetch_t(k):
        at = pl.ds(k * each, each)
        return pltpu.make_async_copy(t_hbm.at[at], t_ref.at[at], t_sems.at[k])

    def fetch_v(d):
        return pltpu.make_async_copy(v_hbm.at[d], v_ref.at[d], v_sems.at[d])

    def put_mine(d):
        return pltpu.make_async_copy(mine_ref.at[d], mine_hbm.at[d], mine_sems.at[d])

    def put_other(d):
        return pltpu.make_async_copy(other_ref.at[d], other_hbm.at[d], other_sems.at[d])

    def own(d, i):
        return ids_ref[d, few, i]

    fetch_ids = pltpu.make_async_copy(
        t_hbm.at[pl.ds(plane_ref[0] * cell, cell), pl.ds(MAIN, 8), pl.ds(0, LANES)], ids_ref, ids_sem
    )
    fetch_pairs = pltpu.make_async_copy(
        t_hbm.at[pl.ds(plane_ref[0] * cell, cell), pl.ds(MAIN, 8), pl.ds(0, LANES)], pairs_ref, pairs_sem
    )
    fetch_few = pltpu.make_async_copy(v_hbm.at[:, :, pl.ds(MAIN * tiles, LANES)], few_ref, few_sem)
    fetch_ids.start()
    fetch_pairs.start()
    fetch_few.start()
    for k in range(chunks):
        fetch_t(k).start()
    for d in range(ahead // 2):
        fetch_v(d).start()
    def apart(value, target):
        zeroth = value * (1.0 - target)
        value = jnp.concatenate([zeroth, value - zeroth], axis=0)
        rest = value - value.astype(jnp.bfloat16).astype(jnp.float32)
        return jnp.concatenate([value, rest], axis=0).astype(jnp.bfloat16)

    fetch_pairs.wait()
    fetch_few.wait()
    for d in range(cell):
        column = jnp.transpose(jnp.broadcast_to(pairs_ref[d, few + 1 : few + 2, :], (LANES, LANES)))
        column = jnp.concatenate([column] * few, axis=1).astype(jnp.int32)
        route = (place == column + which * peers).astype(jnp.float32).astype(jnp.bfloat16)
        both = apart(few_ref[d], pairs_ref[d, few + 2 : few + 3, :])
        routed_ref[d] = jnp.dot(both, route, preferred_element_type=jnp.float32).astype(jnp.bfloat16)
    for k in range(chunks):
        fetch_t(k).wait()
        for s in range(k * each, (k + 1) * each):
            value = t_ref[s, :MAIN, :]
            high = value.astype(jnp.bfloat16)
            high_ref[s] = high
            low_ref[s] = (value - high.astype(jnp.float32)).astype(jnp.bfloat16)
    for e in range(few):
        value = t_ref[:, MAIN + e, :]
        high = value.astype(jnp.bfloat16)
        rest_ref[0, e * peers : (e + 1) * peers, :] = high
        rest_ref[1, e * peers : (e + 1) * peers, :] = (value - high.astype(jnp.float32)).astype(jnp.bfloat16)
    start = jnp.dot(routed_ref[...].reshape(cell * 4 * rows, wide), rest_ref[0], preferred_element_type=jnp.float32)
    start = start.reshape(cell, 4 * rows, wide)
    start = start[:, : 2 * rows] + start[:, 2 * rows :]
    minor = routed_ref[:, : 2 * rows, :].reshape(cell * 2 * rows, wide)
    minor = jnp.dot(minor, rest_ref[1], preferred_element_type=jnp.float32)
    start_ref[...] = start + minor.reshape(cell, 2 * rows, wide)
    for d in range(ahead // 2, ahead):
        fetch_v(d).start()
    fetch_ids.wait()
    is_first = core_ref[0] == 0

    def block(d, _):
        @pl.when(d + ahead < cell)
        def _():
            fetch_v(d + ahead).start()

        fetch_v(d).wait()
        total = contract(d)
        mine_ref[d] = jnp.where(is_first, total[:, :LANES], total[:, LANES:])
        other_ref[d] = jnp.where(is_first, total[:, LANES:], total[:, :LANES])
        put_mine(d).start()
        put_other(d).start()
        return 0

    def contract(d):
        def load(q):
            return v_ref[d, :, q * LANES : (q + 1) * LANES]

        def targets(j):
            first = j * LANES // MAIN
            made = own(d, tiles + first)
            for h in range(first + 1, (j * LANES + LANES - 1) // MAIN + 1):
                made = jnp.where(lane_row < MAIN * h - j * LANES, made, own(d, tiles + h))
            return made

        total = jnp.zeros((4 * rows, wide), jnp.float32)
        minor = start_ref[d]
        for g in range(0, tiles, step):
            span = range(g * MAIN // LANES, (g + step) * MAIN // LANES)
            both = jnp.concatenate([apart(load(j), targets(j)) for j in span], axis=1)
            at = [own(d, h).astype(jnp.int32) for h in range(g, g + step)]
            t_high = jnp.concatenate([high_ref[s] for s in at], axis=0)
            t_low = jnp.concatenate([low_ref[s] for s in at], axis=0)
            total += jnp.dot(both, t_high, preferred_element_type=jnp.float32)
            minor += jnp.dot(both[: 2 * rows], t_low, preferred_element_type=jnp.float32)
        return total[: 2 * rows] + total[2 * rows :] + minor

    lax.fori_loop(0, cell, block, 0)
    for d in range(cell):
        put_mine(d).wait()
        put_other(d).wait()


def ladder(core, plane, got, held, part, step):
    cell, rows, width = got.shape
    peers, padded, wide = held.shape
    chunks = 8
    anywhere = pl.BlockSpec(memory_space=pl.ANY)
    scalar = pl.BlockSpec(memory_space=pltpu.SMEM)
    shape = jax.ShapeDtypeStruct((cell, RD * rows, LANES), jnp.float32)
    return pl.pallas_call(
        functools.partial(ladder_kernel, part, step),
        in_specs=[scalar, scalar, anywhere, anywhere],
        out_specs=[anywhere, anywhere],
        out_shape=(shape, shape),
        scratch_shapes=[
            pltpu.VMEM((cell, rows, width), jnp.float32),
            pltpu.VMEM((peers, padded, wide), jnp.float32),
            pltpu.VMEM((peers, MAIN, wide), jnp.bfloat16),
            pltpu.VMEM((peers, MAIN, wide), jnp.bfloat16),
            pltpu.VMEM((2, (part - MAIN) * peers, wide), jnp.bfloat16),
            pltpu.VMEM((cell, 8, LANES), jnp.float32),
            pltpu.VMEM((cell, rows, LANES), jnp.float32),
            pltpu.VMEM((cell, 4 * rows, (part - MAIN) * peers), jnp.bfloat16),
            pltpu.VMEM((cell, 2 * rows, wide), jnp.float32),
            pltpu.VMEM(shape.shape, jnp.float32),
            pltpu.VMEM(shape.shape, jnp.float32),
            pltpu.SMEM((cell, 8, LANES), jnp.float32),
            pltpu.SemaphoreType.DMA((chunks,)),
            pltpu.SemaphoreType.DMA((cell,)),
            pltpu.SemaphoreType.DMA((cell,)),
            pltpu.SemaphoreType.DMA((cell,)),
            pltpu.SemaphoreType.DMA,
            pltpu.SemaphoreType.DMA,
            pltpu.SemaphoreType.DMA,
        ],
        compiler_params=pltpu.CompilerParams(vmem_limit_bytes=VMEM),
        cost_estimate=pl.CostEstimate(
            flops=12 * rows * got.size // rows * wide * RD, bytes_accessed=4 * (got.size + held.size), transcendentals=0
        ),
    )(core, plane, got, held)


def exchange(value, axes):
    return lax.all_to_all(value, axes, split_axis=0, concat_axis=0, tiled=True)


def body(amplitudes, integrals, tile_map, cd_ids, res_ids):
    cell = lax.axis_size(PLANE)
    tiles, rows, depth = integrals.shape
    wide = amplitudes.shape[1]
    part = depth // cell
    peers = tile_map.shape[0]
    shape = tuple(lax.axis_size(a) for a in TILE)
    own = exchange(pack(tile_map, cd_ids, res_ids, amplitudes[0].T, cell, shape), PLANE)
    sent = cut(integrals, cell)
    own, sent = lax.optimization_barrier((own, sent))
    shared = lax.all_gather(own, "z").reshape(peers, PADDED, wide)
    sent, core, plane = lax.optimization_barrier((sent, lax.axis_index("slab"), lax.axis_index("z")))
    got = exchange(sent, PLANE)
    got, shared, core, plane = lax.optimization_barrier((got, shared, core, plane))
    mine, other = ladder(core[None], plane[None], got, shared, part, 16)
    mine += lax.ppermute(other, "slab", [(0, 1), (1, 0)])
    back = exchange(mine, PLANE)
    return jnp.sum(back, axis=0).reshape(RD, rows, LANES)


def solution(mesh):
    grid = Mesh(mesh.devices.reshape(4, 8, 4, 2), TILE + ("slab",))
    placed = (P(TILE, None, "slab"), P(TILE, None, "slab"), P(), P(TILE), P(TILE))
    return jax.shard_map(
        body, mesh=grid, in_specs=placed, out_specs=P(TILE, None, "slab"), check_vma=False
    )
```
